32 devices in a mesh: groups: 2 (over y), rep: 4 (over x, core), tp: 4 (over z).
Axes of the slice: x: 2, y: 2, z: 4, core: 2. Of those that a mesh axis runs over, the one named last changes fastest.
Arguments:
- activations: bfloat16 [4096, 8192], P(('groups', 'rep'), 'tp'), parts along dimension 0, may hold values from -6 to 6
- row_adapter: int32 [4096, 1], P(('groups', 'rep')), parts along dimension 0, may hold values from 0 to 31; in each aligned block of 512 rows (0 to 511, 512 to 1023, ...) at most 16 rows name the same one
- base_weight: bfloat16 [8192, 4096], P(None, 'tp'), may hold values from -0.0625 to 0.0625
- basis_down: bfloat16 [8192, 256], P('tp'), may hold values from -0.0625 to 0.0625
- adapter_cores: bfloat16 [32, 256, 256], P('rep'), may hold values from -0.375 to 0.375
- basis_up: bfloat16 [256, 4096], P(None, 'tp'), may hold values from -0.375 to 0.375
Outputs:
- queries: bfloat16 [4096, 4096], P(('groups', 'rep'), 'tp'), parts along dimension 0
The draws below stay inside these ranges and needn't reach their ends.
There are 2 independent parts, one for each index of `groups`. The reference program is written for one: setup_inputs(seed, part) draws one part's arguments, and reference() takes and returns one part's arrays. A program takes and returns all parts, laid end to end along the dimension named above; an argument that names none is the same for every part. Nothing has to cross between parts.
Inputs may be any that keep to these rules, and one draw needn't show every extreme that they name: `row_adapter`: in each aligned block of 512 rows (the rows of one replica) no adapter is named by more than 16 rows.
All inputs are finite; a program needn't handle non-finite values.
Results may differ from the reference program's by a relative error of at most 0.0047.
Values may be sent and summed in bfloat16 or wider, within the bound.
No kernel may reach another device: no remote copies, remote signals or barrier semaphores. Data moves between devices by JAX's collectives and lax.ppermute only.
A program may use at most 128 MiB of HBM per device.

```python
import math
import jax
import jax.numpy as jnp
import numpy as np
from jax import lax

D = 8192
Q = 4096
R = 256
BLK = 16
TOK_DEV = 512
ADAPTERS = 32
TOKENS = 2048


def shard_levels(rng, extent, pieces, least, top_value):
    factor_of = 1.0
    for position, parts in pieces:
        draws = jax.random.uniform(jax.random.fold_in(jax.random.fold_in(rng, 6), position), (parts,), jnp.float32, least / len(pieces), top_value / len(pieces))
        factor_of = factor_of * jnp.repeat(jnp.exp(draws), extent[position] // parts).reshape((-1,) + (1,) * (len(extent) - 1 - position))
    return factor_of


def deal_out(key, own, number, rows, number_of, top, limit, skew):
    ranking = jax.random.permutation(key, number_of)
    heavy_load, ordinary = load_shares(number_of, rows * top, limit, skew, True), load_shares(number_of, rows * top, limit, skew, False)
    places = jnp.arange(number_of)

    def named(sizes, turn):
        used = int((sizes > 0).sum())
        fixed = max(1, used // 4)
        shifted = fixed + (places - fixed + turn * (used - fixed)) % max(1, number_of - fixed)
        return jnp.zeros((number_of,), jnp.int32).at[ranking[jnp.where(places < fixed, places, shifted)]].set(jnp.asarray(sizes, jnp.int32))

    sizes = jnp.where(number % 4 == 0, named(heavy_load, number // 4), named(ordinary, number - number // 4 - 1))
    mixed = jax.random.permutation(jax.random.fold_in(own, 3), number_of)
    source_of, taker = mixed[0:number_of // 2 * 2:2], mixed[1:number_of // 2 * 2:2]
    room = jnp.minimum(sizes[source_of] - 1, limit - sizes[taker]) // 2
    room = jnp.where((source_of == ranking[0]) | (taker == ranking[0]) | (sizes[taker] == 0), 0, jnp.maximum(room, 0))
    shifted = jax.random.randint(jax.random.fold_in(own, 4), (number_of // 2,), 0, 1 << 20) % (room + 1)
    sizes = sizes.at[source_of].add(-shifted).at[taker].add(shifted)
    members = jnp.searchsorted(jnp.cumsum(sizes), jnp.arange(rows * top), side="right").astype(jnp.int32)
    grid = members.reshape(top, rows).T
    grid = grid[jax.random.permutation(jax.random.fold_in(own, 1), rows)]
    turn = jax.random.randint(jax.random.fold_in(own, 2), (rows, 1), 0, top)
    return jnp.take_along_axis(grid, (jnp.arange(top)[None, :] + turn) % top, axis=1)


def load_shares(count, total, bound, slope, full):
    loads = [(1 << 20) // math.isqrt(standing ** slope) + 1 for standing in range(1, count + 1)]
    largest = bound if full else min(bound, max(-(-total // count), total * loads[0] // sum(loads)))
    least = 1 if total - largest >= count - 1 else 0
    given, rest = [largest] + [least] * (count - 1), total - largest - least * (count - 1)
    while rest > 0:
        movable = [i for i in range(1, count) if given[i] < largest] or [i for i in range(1, count) if given[i] < bound]
        mass, budget = sum([loads[i] for i in movable]), rest
        for i in movable:
            addition = min(bound - given[i], max(1, budget * loads[i] // mass), rest)
            given[i] = given[i] + addition
            rest = rest - addition
    return np.array(given)


def scatter_about(key, extent, scale, limit, shards=(), dtype=jnp.bfloat16):
    loudness = shard_levels(key, extent, shards, -0.22, 0.18) if shards else 1.0
    entries = jax.random.normal(key, extent, jnp.float32) * scale * loudness
    return jnp.minimum(jnp.maximum(entries, -limit), limit).astype(dtype)


def setup_inputs(seed: int = 0, part: int = 0) -> dict:
    splits = jax.random.split(jax.random.key(seed), 7)
    part_splits = jax.random.split(jax.random.fold_in(splits[6], part), 7)
    activations = scatter_about(part_splits[0], (TOKENS, D), 1.0, 6.0, ((0, 4), (1, 4)))
    row_adapter_keys = jax.random.split(jax.random.fold_in(part_splits[1], 1), TOKENS // TOK_DEV)
    row_adapter_turns = jax.random.permutation(jax.random.fold_in(part_splits[1], 3), TOKENS // TOK_DEV)
    row_adapter = jax.vmap(lambda own, number: deal_out(jax.random.fold_in(part_splits[1], 2), own, number, TOK_DEV, ADAPTERS, 1, BLK, 2))(row_adapter_keys, row_adapter_turns).reshape((TOKENS, 1))
    base_weight = scatter_about(splits[2], (D, Q), D ** -0.5, 0.0625, ((1, 4),))
    basis_down = scatter_about(splits[3], (D, R), D ** -0.5, 0.0625, ((0, 4),))
    adapter_cores = scatter_about(splits[4], (ADAPTERS, R, R), R ** -0.5, 0.375, ((0, 4),))
    basis_up = scatter_about(splits[5], (R, Q), R ** -0.5, 0.375, ((1, 4),))
    return dict(activations=activations, row_adapter=row_adapter, base_weight=base_weight, basis_down=basis_down, adapter_cores=adapter_cores, basis_up=basis_up)


def reference(activations, row_adapter, base_weight, basis_down, adapter_cores, basis_up):
    base = jnp.dot(activations, base_weight, preferred_element_type=jnp.float32)
    coded = jnp.dot(activations, basis_down, preferred_element_type=jnp.float32).astype(jnp.bfloat16)
    count = coded.shape[0]
    width = coded.shape[1]
    stride = math.gcd(count, 128)
    adapter_ids = row_adapter[:, 0].astype(jnp.int32)

    def mix_block(pair):
        rows, chosen = pair
        cores = jnp.take(adapter_cores, chosen, axis=0).astype(jnp.float32)
        return jnp.einsum("sr,srq->sq", rows.astype(jnp.float32), cores).astype(jnp.bfloat16)

    mixed = lax.map(mix_block, (coded.reshape(count // stride, stride, width), adapter_ids.reshape(count // stride, stride)))
    mixed = mixed.reshape(count, width)
    return (base + jnp.dot(mixed, basis_up, preferred_element_type=jnp.float32)).astype(jnp.bfloat16)
```

```python
import functools

import jax
import jax.numpy as jnp
from jax import lax
from jax.experimental import pallas as pl
from jax.experimental.pallas import tpu as pltpu
from jax.sharding import PartitionSpec as P

BLK = 16


def dot(a, b):
    return jnp.dot(a, b, preferred_element_type=jnp.float32)


def shift(x, axis, by):
    n = lax.axis_size(axis)
    return lax.ppermute(x, axis, [(i, (i + by) % n) for i in range(n)])


def mix_kernel(ids_ref, coded_ref, cores_ref, mixed_ref, slots_ref):
    rows = coded_ref.shape[0]
    adapters = cores_ref.shape[0]
    ids = ids_ref[...]
    named = ids == lax.broadcasted_iota(jnp.int32, (rows, adapters), 1)
    below = lax.broadcasted_iota(jnp.int32, (rows, rows), 0) > lax.broadcasted_iota(
        jnp.int32, (rows, rows), 1
    )
    earlier = dot(below.astype(jnp.bfloat16), named.astype(jnp.bfloat16))
    within = jnp.sum(jnp.where(named, earlier, 0.0), axis=1, keepdims=True).astype(jnp.int32)
    slot = ids * BLK + within
    place = (slot == lax.broadcasted_iota(jnp.int32, (rows, adapters * BLK), 1)).astype(
        jnp.bfloat16
    )
    packed = lax.dot_general(
        place, coded_ref[...], (((0,), (0,)), ((), ())), preferred_element_type=jnp.float32
    ).astype(jnp.bfloat16)
    for a in range(adapters):
        slots_ref[a * BLK : (a + 1) * BLK, :] = dot(
            packed[a * BLK : (a + 1) * BLK, :], cores_ref[a]
        ).astype(jnp.bfloat16)
    mixed_ref[...] = dot(place, slots_ref[...]).astype(jnp.bfloat16)


def mix(ids, coded, cores):
    rows, width = coded.shape
    adapters = cores.shape[0]
    return pl.pallas_call(
        mix_kernel,
        out_shape=jax.ShapeDtypeStruct((rows, width), jnp.bfloat16),
        scratch_shapes=[pltpu.VMEM((adapters * BLK, width), jnp.bfloat16)],
        compiler_params=pltpu.CompilerParams(vmem_limit_bytes=32 * 2**20),
        cost_estimate=pl.CostEstimate(
            flops=2 * rows * width * (3 * adapters * BLK),
            bytes_accessed=cores.size * 2 + rows * width * 4,
            transcendentals=0,
        ),
        name="mix",
    )(ids, coded, cores)


def all_cores(cores):
    rep = lax.axis_index("rep")
    core, x = rep % 2, rep // 2
    mate = lax.ppermute(cores, "rep", [(i, i ^ 1) for i in range(4)])
    across = lax.ppermute(cores, "rep", [(i, i ^ 2) for i in range(4)])
    corner = lax.ppermute(across, "rep", [(i, i ^ 1) for i in range(4)])
    held = [cores, mate, across, corner]

    def from_rep(r):
        other = rep ^ r
        return lax.select_n(other, *held)

    return jnp.concatenate([from_rep(r) for r in range(4)], axis=0)


def on_line(activations, row_adapter, base_weight, basis_down, adapter_cores, basis_up):
    me = lax.axis_index("tp")
    depth = activations.shape[1]
    half = activations.shape[0] // 2

    def weight_of(owner):
        return lax.dynamic_slice_in_dim(base_weight, (owner % 4) * depth, depth, 0)

    partial_value = dot(activations, basis_down)
    top, bottom = activations[:half], activations[half:]
    right_top = shift(top, "tp", 1)
    left_bottom = shift(bottom, "tp", -1)
    right_bottom = shift(bottom, "tp", 1)
    left_top = shift(top, "tp", -1)
    far_top = shift(right_top, "tp", 1)
    far_bottom = shift(left_bottom, "tp", -1)

    pair = partial_value + lax.ppermute(partial_value, "tp", [(0, 1), (1, 0), (2, 3), (3, 2)])
    total = pair + lax.ppermute(pair, "tp", [(0, 3), (3, 0), (1, 2), (2, 1)])
    coded = total.astype(jnp.bfloat16)
    mixed = mix(row_adapter, coded, all_cores(adapter_cores))

    base = dot(activations, weight_of(me)) + dot(mixed, basis_up)
    base = base + dot(jnp.concatenate([right_top, right_bottom], 0), weight_of(me + 3))
    base = base + dot(jnp.concatenate([left_top, left_bottom], 0), weight_of(me + 1))
    base = base + dot(jnp.concatenate([far_top, far_bottom], 0), weight_of(me + 2))
    return base.astype(jnp.bfloat16)


def on_any(activations, row_adapter, base_weight, basis_down, adapter_cores, basis_up):
    width = basis_down.shape[1]
    local_count = adapter_cores.shape[0]
    owners = lax.axis_size("rep")
    all_adapters = local_count * owners
    slot_count = all_adapters * BLK
    base = dot(lax.all_gather(activations, "tp", axis=1, tiled=True), base_weight)
    partial_value = dot(activations, basis_down)
    adapter_ids = row_adapter[:, 0]
    onehot = (adapter_ids[:, None] == jnp.arange(all_adapters, dtype=jnp.int32)[None, :]).astype(
        jnp.int32
    )
    earlier = jnp.cumsum(onehot, axis=0) - onehot
    within = jnp.sum(earlier * onehot, axis=1)
    slot_index = adapter_ids * BLK + within
    coded = lax.psum(partial_value, "tp").astype(jnp.bfloat16)
    packed = jnp.zeros((slot_count, width), jnp.bfloat16).at[slot_index].set(coded)
    packed = packed.reshape(owners, local_count, BLK, width)
    mixed_slots = jnp.einsum(
        "nasr,arq->nasq",
        lax.all_to_all(packed, "rep", split_axis=0, concat_axis=0, tiled=True),
        adapter_cores,
        preferred_element_type=jnp.float32,
    ).astype(jnp.bfloat16)
    returned = lax.all_to_all(mixed_slots, "rep", split_axis=0, concat_axis=0, tiled=True).reshape(
        slot_count, width
    )
    mixed = returned[slot_index]
    return (base + dot(mixed, basis_up)).astype(jnp.bfloat16)


def solution(mesh):
    placed = (
        P(("groups", "rep"), "tp"),
        P(("groups", "rep"), None),
        P(None, "tp"),
        P("tp", None),
        P("rep", None, None),
        P(None, "tp"),
    )
    short = mesh.shape["tp"] == 4 and mesh.shape["rep"] == 4
    return jax.shard_map(
        on_line if short else on_any,
        mesh=mesh,
        in_specs=placed,
        out_specs=P(("groups", "rep"), "tp"),
        check_vma=False,
    )
```

```python
import functools

import jax
import jax.numpy as jnp
from jax import lax
from jax.experimental import pallas as pl
from jax.experimental.pallas import tpu as pltpu
from jax.sharding import PartitionSpec as P

BLK = 16


def dot(a, b):
    return jnp.dot(a, b, preferred_element_type=jnp.float32)


def mix_kernel(ids_ref, coded_ref, cores_ref, mixed_ref, slots_ref):
    rows = coded_ref.shape[0]
    adapters = cores_ref.shape[0]
    ids = ids_ref[...]
    named = ids == lax.broadcasted_iota(jnp.int32, (rows, adapters), 1)
    below = lax.broadcasted_iota(jnp.int32, (rows, rows), 0) > lax.broadcasted_iota(
        jnp.int32, (rows, rows), 1
    )
    earlier = dot(below.astype(jnp.bfloat16), named.astype(jnp.bfloat16))
    within = jnp.sum(jnp.where(named, earlier, 0.0), axis=1, keepdims=True).astype(jnp.int32)
    slot = ids * BLK + within
    place = (slot == lax.broadcasted_iota(jnp.int32, (rows, adapters * BLK), 1)).astype(
        jnp.bfloat16
    )
    packed = lax.dot_general(
        place, coded_ref[...], (((0,), (0,)), ((), ())), preferred_element_type=jnp.float32
    ).astype(jnp.bfloat16)
    for a in range(adapters):
        slots_ref[a * BLK : (a + 1) * BLK, :] = dot(
            packed[a * BLK : (a + 1) * BLK, :], cores_ref[a]
        ).astype(jnp.bfloat16)
    mixed_ref[...] = dot(place, slots_ref[...]).astype(jnp.bfloat16)


def mix(ids, coded, cores):
    rows, width = coded.shape
    adapters = cores.shape[0]
    return pl.pallas_call(
        mix_kernel,
        out_shape=jax.ShapeDtypeStruct((rows, width), jnp.bfloat16),
        scratch_shapes=[pltpu.VMEM((adapters * BLK, width), jnp.bfloat16)],
        compiler_params=pltpu.CompilerParams(vmem_limit_bytes=32 * 2**20),
        cost_estimate=pl.CostEstimate(
            flops=2 * rows * width * (3 * adapters * BLK),
            bytes_accessed=cores.size * 2 + rows * width * 4,
            transcendentals=0,
        ),
        name="mix",
    )(ids, coded, cores)


def lend_kernel(spot_ref, x_ref, *rest, blocks, width):
    count = 1 + max(b[0] for b in blocks)
    weights, out_ref = rest[:count], rest[-1]
    add_ref = rest[count] if len(rest) > count + 1 else None
    spot = spot_ref[0]
    pieces = sum(len(b[2]) for b in blocks)
    piece = x_ref.shape[1] // pieces
    columns = [
        jnp.concatenate(
            [x_ref[:, pl.ds(pl.multiple_of((spot ^ m) * piece, piece), piece)] for m in masks],
            axis=1,
        )
        for _, _, masks in blocks
    ]
    for n in range(0, out_ref.shape[1], width):
        part = slice(n, n + width)
        value = 0.0 if add_ref is None else add_ref[:, part]
        for x, (operand, row, masks) in zip(columns, blocks):
            value = value + dot(x, weights[operand][row : row + piece * len(masks), part])
        out_ref[:, part] = value.astype(out_ref.dtype)


def lend(spot, x, weights, blocks, add, dtype, name):
    rows, depth = x.shape
    columns = weights[0].shape[1]
    whole = pl.BlockSpec(memory_space=pltpu.VMEM)
    operands = (spot.reshape(1), x, *weights) + (() if add is None else (add,))
    return pl.pallas_call(
        functools.partial(lend_kernel, blocks=blocks, width=256),
        out_shape=jax.ShapeDtypeStruct((rows, columns), dtype),
        in_specs=[pl.BlockSpec(memory_space=pltpu.SMEM)] + [whole] * (len(operands) - 1),
        out_specs=whole,
        compiler_params=pltpu.CompilerParams(vmem_limit_bytes=24 * 2**20),
        cost_estimate=pl.CostEstimate(
            flops=2 * rows * depth * columns,
            bytes_accessed=depth * columns * 2 + rows * (depth + columns) * 2,
            transcendentals=0,
        ),
        name=name,
    )(*operands)


def all_cores(cores, ahead):
    rep = lax.axis_index("rep")
    core, x = rep % 2, rep // 2
    mate = lax.ppermute(cores, "rep", [(i, i ^ 1) for i in range(4)])
    across = lax.ppermute(cores, "rep", [(i, i ^ 2) for i in range(4)])
    across, mate, ahead = lax.optimization_barrier((across, mate, ahead))
    corner = lax.ppermute(across, "rep", [(i, i ^ 1) for i in range(4)])
    held = [cores, mate, across, corner]

    def from_rep(r):
        other = rep ^ r
        return lax.select_n(other, *held)

    return jnp.concatenate([from_rep(r) for r in range(4)], axis=0), ahead


IN = [(0, 1), (3, 2)]
OUT = [(1, 0), (2, 3)]
SWAP = [(1, 2), (2, 1)]


def send(x, pairs):
    return lax.ppermute(x, "tp", pairs)


def swap_rep(x, bit):
    return lax.ppermute(x, "rep", [(i, i ^ bit) for i in range(4)])


def swap_groups(x):
    return lax.ppermute(x, "groups", [(0, 1), (1, 0)])


def on_line(activations, row_adapter, base_weight, basis_down, adapter_cores, basis_up):
    me = lax.axis_index("tp")
    inner = (me == 1) | (me == 2)
    left = me < 2
    near_in, far_in = jnp.where(left, 1, 2), jnp.where(left, 2, 1)
    near_out, far_out = jnp.where(left, 0, 3), jnp.where(left, 3, 0)
    spot = lax.axis_index("groups") * 4 + lax.axis_index("rep")
    rows, depth = activations.shape
    piece = depth // 8
    cuts = (0, rows // 2, rows * 3 // 4, rows)
    parts = [slice(a, b) for a, b in zip(cuts, cuts[1:])]

    def weight_of(owner):
        return lax.dynamic_slice_in_dim(base_weight, owner * depth, depth, 0)

    def piece_of(owner):
        return lax.dynamic_slice_in_dim(base_weight, owner * depth + spot * piece, piece, 0)

    pieces = send(jnp.concatenate([piece_of(near_in), piece_of(far_out)], axis=0), IN)
    first = send(activations[: rows // 2], SWAP)
    partial_value = dot(activations, basis_down)
    side = partial_value + send(partial_value, IN)
    cores, _ = all_cores(adapter_cores, first)
    second, first = lax.optimization_barrier((activations[rows // 2 :], first))
    second = send(second, SWAP)

    near, far = pieces[:piece], pieces[piece:]
    near = jnp.concatenate([near, swap_groups(near)], axis=0)
    far = jnp.concatenate([far, swap_rep(far, 2)], axis=0)
    near, far, cores = lax.optimization_barrier((near, far, cores))
    near_more, far_more = swap_rep(near, 2), swap_groups(far)
    mate = swap_rep(jnp.concatenate([near, far], axis=0), 1)
    mate_more = swap_rep(jnp.concatenate([near_more, far_more], axis=0), 1)
    two = 2 * piece
    near_blocks = ((0, 0, (0, 4)), (1, 0, (2, 6)), (2, 0, (1, 5)), (3, 0, (3, 7)))
    far_blocks = ((0, 0, (0, 2)), (1, 0, (4, 6)), (2, two, (1, 3)), (3, two, (5, 7)))

    received = jnp.concatenate([first, second], axis=0)
    turned = [send(jnp.where(inner, received[p], activations[p]), IN + OUT) for p in parts]
    half, turned[0] = lax.optimization_barrier((side.astype(jnp.bfloat16), turned[0]))
    coded = (side + send(half, SWAP).astype(jnp.float32)).astype(jnp.bfloat16)
    coded, turned[1] = lax.optimization_barrier((coded, turned[1]))
    coded = jnp.where(inner, coded, send(coded, OUT))
    mixed = mix(row_adapter, coded, cores)

    base = dot(activations, weight_of(me)) + dot(mixed, basis_up)
    base = base + dot(received, weight_of(far_in))
    base = base + dot(jnp.concatenate(turned, 0), weight_of(jnp.where(inner, near_out, far_in)))
    lent = lend(
        spot, activations, (near, near_more, mate, mate_more), near_blocks, None, jnp.float32,
        "lend_near",
    )
    last_weight = weight_of(far_out)
    crossed, sent = [], []
    for i, p in enumerate(parts):
        x = turned[i]
        if i > 1:
            x, sent[i - 2] = lax.optimization_barrier((x, sent[i - 2]))
        crossed.append(send(x, SWAP))
        x = crossed[i]
        if i:
            x, sent[i - 1] = lax.optimization_barrier((x, sent[i - 1]))
        weights = (far, far_more, mate, mate_more)
        sent.append(lend(spot, x, weights, far_blocks, lent[p], jnp.bfloat16, "lend_far"))
    out = []
    for p, x, y in zip(parts, crossed, sent):
        whole = base[p] + dot(x, last_weight) + send(y, OUT).astype(jnp.float32)
        out.append(whole.astype(jnp.bfloat16))
    return jnp.concatenate(out, axis=0)


def on_any(activations, row_adapter, base_weight, basis_down, adapter_cores, basis_up):
    width = basis_down.shape[1]
    local_count = adapter_cores.shape[0]
    owners = lax.axis_size("rep")
    all_adapters = local_count * owners
    slot_count = all_adapters * BLK
    base = dot(lax.all_gather(activations, "tp", axis=1, tiled=True), base_weight)
    partial_value = dot(activations, basis_down)
    adapter_ids = row_adapter[:, 0]
    onehot = (adapter_ids[:, None] == jnp.arange(all_adapters, dtype=jnp.int32)[None, :]).astype(
        jnp.int32
    )
    earlier = jnp.cumsum(onehot, axis=0) - onehot
    within = jnp.sum(earlier * onehot, axis=1)
    slot_index = adapter_ids * BLK + within
    coded = lax.psum(partial_value, "tp").astype(jnp.bfloat16)
    packed = jnp.zeros((slot_count, width), jnp.bfloat16).at[slot_index].set(coded)
    packed = packed.reshape(owners, local_count, BLK, width)
    mixed_slots = jnp.einsum(
        "nasr,arq->nasq",
        lax.all_to_all(packed, "rep", split_axis=0, concat_axis=0, tiled=True),
        adapter_cores,
        preferred_element_type=jnp.float32,
    ).astype(jnp.bfloat16)
    returned = lax.all_to_all(mixed_slots, "rep", split_axis=0, concat_axis=0, tiled=True).reshape(
        slot_count, width
    )
    mixed = returned[slot_index]
    return (base + dot(mixed, basis_up)).astype(jnp.bfloat16)


def solution(mesh):
    placed = (
        P(("groups", "rep"), "tp"),
        P(("groups", "rep"), None),
        P(None, "tp"),
        P("tp", None),
        P("rep", None, None),
        P(None, "tp"),
    )
    short = (mesh.shape["groups"], mesh.shape["rep"], mesh.shape["tp"]) == (2, 4, 4)
    return jax.shard_map(
        on_line if short else on_any,
        mesh=mesh,
        in_specs=placed,
        out_specs=P(("groups", "rep"), "tp"),
        check_vma=False,
    )
```

```python
import functools

import jax
import jax.numpy as jnp
from jax import lax
from jax.experimental import pallas as pl
from jax.experimental.pallas import tpu as pltpu
from jax.sharding import PartitionSpec as P

BLK = 16


def dot(a, b):
    return jnp.dot(a, b, preferred_element_type=jnp.float32)


def mix_kernel(ids_ref, coded_ref, cores_ref, mixed_ref, slots_ref):
    rows = coded_ref.shape[0]
    adapters = cores_ref.shape[0]
    ids = ids_ref[...]
    named = ids == lax.broadcasted_iota(jnp.int32, (rows, adapters), 1)
    below = lax.broadcasted_iota(jnp.int32, (rows, rows), 0) > lax.broadcasted_iota(
        jnp.int32, (rows, rows), 1
    )
    earlier = dot(below.astype(jnp.bfloat16), named.astype(jnp.bfloat16))
    within = jnp.sum(jnp.where(named, earlier, 0.0), axis=1, keepdims=True).astype(jnp.int32)
    slot = ids * BLK + within
    place = (slot == lax.broadcasted_iota(jnp.int32, (rows, adapters * BLK), 1)).astype(
        jnp.bfloat16
    )
    packed = lax.dot_general(
        place, coded_ref[...], (((0,), (0,)), ((), ())), preferred_element_type=jnp.float32
    ).astype(jnp.bfloat16)
    for a in range(adapters):
        slots_ref[a * BLK : (a + 1) * BLK, :] = dot(
            packed[a * BLK : (a + 1) * BLK, :], cores_ref[a]
        ).astype(jnp.bfloat16)
    mixed_ref[...] = dot(place, slots_ref[...]).astype(jnp.bfloat16)


def mix(ids, coded, cores):
    rows, width = coded.shape
    adapters = cores.shape[0]
    return pl.pallas_call(
        mix_kernel,
        out_shape=jax.ShapeDtypeStruct((rows, width), jnp.bfloat16),
        scratch_shapes=[pltpu.VMEM((adapters * BLK, width), jnp.bfloat16)],
        compiler_params=pltpu.CompilerParams(vmem_limit_bytes=32 * 2**20),
        cost_estimate=pl.CostEstimate(
            flops=2 * rows * width * (3 * adapters * BLK),
            bytes_accessed=cores.size * 2 + rows * width * 4,
            transcendentals=0,
        ),
        name="mix",
    )(ids, coded, cores)


def lend_kernel(spot_ref, x_ref, *rest, blocks, width):
    count = 1 + max(b[0] for b in blocks)
    weights, out_ref = rest[:count], rest[-1]
    add_ref = rest[count] if len(rest) > count + 1 else None
    spot = spot_ref[0]
    pieces = sum(len(b[2]) for b in blocks)
    piece = x_ref.shape[1] // pieces
    columns = [
        jnp.concatenate(
            [x_ref[:, pl.ds(pl.multiple_of((spot ^ m) * piece, piece), piece)] for m in masks],
            axis=1,
        )
        for _, _, masks in blocks
    ]
    for n in range(0, out_ref.shape[1], width):
        part = slice(n, n + width)
        value = 0.0 if add_ref is None else add_ref[:, part]
        for x, (operand, row, masks) in zip(columns, blocks):
            value = value + dot(x, weights[operand][row : row + piece * len(masks), part])
        out_ref[:, part] = value.astype(out_ref.dtype)


def lend(spot, x, weights, blocks, add, dtype, name):
    rows, depth = x.shape
    columns = weights[0].shape[1]
    whole = pl.BlockSpec(memory_space=pltpu.VMEM)
    operands = (spot.reshape(1), x, *weights) + (() if add is None else (add,))
    return pl.pallas_call(
        functools.partial(lend_kernel, blocks=blocks, width=256),
        out_shape=jax.ShapeDtypeStruct((rows, columns), dtype),
        in_specs=[pl.BlockSpec(memory_space=pltpu.SMEM)] + [whole] * (len(operands) - 1),
        out_specs=whole,
        compiler_params=pltpu.CompilerParams(vmem_limit_bytes=24 * 2**20),
        cost_estimate=pl.CostEstimate(
            flops=2 * rows * depth * columns,
            bytes_accessed=depth * columns * 2 + rows * (depth + columns) * 2,
            transcendentals=0,
        ),
        name=name,
    )(*operands)


def all_cores(cores):
    rep = lax.axis_index("rep")
    core, x = rep % 2, rep // 2
    mate = lax.ppermute(cores, "rep", [(i, i ^ 1) for i in range(4)])
    across = lax.ppermute(cores, "rep", [(i, i ^ 2) for i in range(4)])
    across, mate = lax.optimization_barrier((across, mate))
    corner = lax.ppermute(across, "rep", [(i, i ^ 1) for i in range(4)])
    held = [cores, mate, across, corner]

    def from_rep(r):
        other = rep ^ r
        return lax.select_n(other, *held)

    return jnp.concatenate([from_rep(r) for r in range(4)], axis=0)


IN = [(0, 1), (3, 2)]
OUT = [(1, 0), (2, 3)]
SWAP = [(1, 2), (2, 1)]


def send(x, pairs):
    return lax.ppermute(x, "tp", pairs)


def swap_rep(x, bit):
    return lax.ppermute(x, "rep", [(i, i ^ bit) for i in range(4)])


def swap_groups(x):
    return lax.ppermute(x, "groups", [(0, 1), (1, 0)])


def on_line(activations, row_adapter, base_weight, basis_down, adapter_cores, basis_up):
    me = lax.axis_index("tp")
    inner = (me == 1) | (me == 2)
    left = me < 2
    near_in, far_in = jnp.where(left, 1, 2), jnp.where(left, 2, 1)
    near_out, far_out = jnp.where(left, 0, 3), jnp.where(left, 3, 0)
    spot = lax.axis_index("groups") * 4 + lax.axis_index("rep")
    rows, depth = activations.shape
    piece = depth // 8
    cuts = (0, rows // 2, rows * 3 // 4, rows)
    parts = [slice(a, b) for a, b in zip(cuts, cuts[1:])]

    def weight_of(owner):
        return lax.dynamic_slice_in_dim(base_weight, owner * depth, depth, 0)

    def piece_of(owner):
        return lax.dynamic_slice_in_dim(base_weight, owner * depth + spot * piece, piece, 0)

    swapped = send(activations, SWAP)
    pieces = send(jnp.concatenate([piece_of(far_in), piece_of(far_out)], axis=0), IN)
    partial_value = dot(activations, basis_down)
    side = send(partial_value.astype(jnp.bfloat16), IN).astype(jnp.float32) + partial_value
    whole = side + send(side.astype(jnp.bfloat16), SWAP).astype(jnp.float32)
    coded = whole.astype(jnp.bfloat16)
    cores = all_cores(adapter_cores)

    near, far = pieces[:piece], pieces[piece:]
    top, near = lax.optimization_barrier((activations[: rows // 2], near))
    turned = [send(top, IN + OUT)]
    near = jnp.concatenate([near, swap_groups(near)], axis=0)
    far = jnp.concatenate([far, swap_rep(far, 2)], axis=0)
    near, far, cores = lax.optimization_barrier((near, far, cores))
    near_more, far_more = swap_rep(near, 2), swap_groups(far)
    near_weights = (near, near_more, swap_rep(near, 1), swap_rep(near_more, 1))
    far_weights = (far, far_more, swap_rep(far, 1), swap_rep(far_more, 1))
    near_blocks = ((0, 0, (0, 4)), (1, 0, (2, 6)), (2, 0, (1, 5)), (3, 0, (3, 7)))
    far_blocks = ((0, 0, (0, 2)), (1, 0, (4, 6)), (2, 0, (1, 3)), (3, 0, (5, 7)))

    bottom, turned[0], swapped, coded = lax.optimization_barrier(
        (activations[rows // 2 :], turned[0], swapped, coded)
    )
    coded = jnp.where(inner, coded, send(coded, OUT))
    turned.append(send(bottom, IN + OUT))
    mixed = mix(row_adapter, coded, cores)

    base = dot(activations, weight_of(me)) + dot(mixed, basis_up)
    base = base + dot(swapped, weight_of(far_in))
    base = base + dot(
        jnp.concatenate(turned, 0), weight_of(jnp.where(inner, near_out, near_in))
    )
    lent = lend(spot, swapped, near_weights, near_blocks, None, jnp.float32, "lend_near")
    last_weight = weight_of(far_out)
    crossed, sent = [], []
    for i, p in enumerate(parts):
        x = turned[0] if i == 0 else turned[1][p.start - rows // 2 : p.stop - rows // 2]
        if i > 1:
            x, sent[i - 2] = lax.optimization_barrier((x, sent[i - 2]))
        crossed.append(send(x, SWAP))
        x = crossed[i]
        if i:
            x, sent[i - 1] = lax.optimization_barrier((x, sent[i - 1]))
        sent.append(lend(spot, x, far_weights, far_blocks, lent[p], jnp.bfloat16, "lend_far"))
    out, back = [], None
    for p, x, y in zip(parts, crossed, sent):
        if back is not None:
            y, back = lax.optimization_barrier((y, back))
        back = send(y, OUT)
        out.append((base[p] + dot(x, last_weight) + back.astype(jnp.float32)).astype(jnp.bfloat16))
    return jnp.concatenate(out, axis=0)


def on_any(activations, row_adapter, base_weight, basis_down, adapter_cores, basis_up):
    width = basis_down.shape[1]
    local_count = adapter_cores.shape[0]
    owners = lax.axis_size("rep")
    all_adapters = local_count * owners
    slot_count = all_adapters * BLK
    base = dot(lax.all_gather(activations, "tp", axis=1, tiled=True), base_weight)
    partial_value = dot(activations, basis_down)
    adapter_ids = row_adapter[:, 0]
    onehot = (adapter_ids[:, None] == jnp.arange(all_adapters, dtype=jnp.int32)[None, :]).astype(
        jnp.int32
    )
    earlier = jnp.cumsum(onehot, axis=0) - onehot
    within = jnp.sum(earlier * onehot, axis=1)
    slot_index = adapter_ids * BLK + within
    coded = lax.psum(partial_value, "tp").astype(jnp.bfloat16)
    packed = jnp.zeros((slot_count, width), jnp.bfloat16).at[slot_index].set(coded)
    packed = packed.reshape(owners, local_count, BLK, width)
    mixed_slots = jnp.einsum(
        "nasr,arq->nasq",
        lax.all_to_all(packed, "rep", split_axis=0, concat_axis=0, tiled=True),
        adapter_cores,
        preferred_element_type=jnp.float32,
    ).astype(jnp.bfloat16)
    returned = lax.all_to_all(mixed_slots, "rep", split_axis=0, concat_axis=0, tiled=True).reshape(
        slot_count, width
    )
    mixed = returned[slot_index]
    return (base + dot(mixed, basis_up)).astype(jnp.bfloat16)


def solution(mesh):
    placed = (
        P(("groups", "rep"), "tp"),
        P(("groups", "rep"), None),
        P(None, "tp"),
        P("tp", None),
        P("rep", None, None),
        P(None, "tp"),
    )
    short = (mesh.shape["groups"], mesh.shape["rep"], mesh.shape["tp"]) == (2, 4, 4)
    return jax.shard_map(
        on_line if short else on_any,
        mesh=mesh,
        in_specs=placed,
        out_specs=P(("groups", "rep"), "tp"),
        check_vma=False,
    )
```

```python
import functools

import jax
import jax.numpy as jnp
from jax import lax
from jax.experimental import pallas as pl
from jax.experimental.pallas import tpu as pltpu
from jax.sharding import PartitionSpec as P

BLK = 16


def dot(a, b):
    return jnp.dot(a, b, preferred_element_type=jnp.float32)


def mix_kernel(ids_ref, coded_ref, cores_ref, mixed_ref, slots_ref):
    rows = coded_ref.shape[0]
    adapters = cores_ref.shape[0]
    ids = ids_ref[...]
    named = ids == lax.broadcasted_iota(jnp.int32, (rows, adapters), 1)
    below = lax.broadcasted_iota(jnp.int32, (rows, rows), 0) > lax.broadcasted_iota(
        jnp.int32, (rows, rows), 1
    )
    earlier = dot(below.astype(jnp.bfloat16), named.astype(jnp.bfloat16))
    within = jnp.sum(jnp.where(named, earlier, 0.0), axis=1, keepdims=True).astype(jnp.int32)
    slot = ids * BLK + within
    place = (slot == lax.broadcasted_iota(jnp.int32, (rows, adapters * BLK), 1)).astype(
        jnp.bfloat16
    )
    packed = lax.dot_general(
        place, coded_ref[...], (((0,), (0,)), ((), ())), preferred_element_type=jnp.float32
    ).astype(jnp.bfloat16)
    for a in range(adapters):
        slots_ref[a * BLK : (a + 1) * BLK, :] = dot(
            packed[a * BLK : (a + 1) * BLK, :], cores_ref[a]
        ).astype(jnp.bfloat16)
    mixed_ref[...] = dot(place, slots_ref[...]).astype(jnp.bfloat16)


def mix(ids, coded, cores):
    rows, width = coded.shape
    adapters = cores.shape[0]
    return pl.pallas_call(
        mix_kernel,
        out_shape=jax.ShapeDtypeStruct((rows, width), jnp.bfloat16),
        scratch_shapes=[pltpu.VMEM((adapters * BLK, width), jnp.bfloat16)],
        compiler_params=pltpu.CompilerParams(vmem_limit_bytes=32 * 2**20),
        cost_estimate=pl.CostEstimate(
            flops=2 * rows * width * (3 * adapters * BLK),
            bytes_accessed=cores.size * 2 + rows * width * 4,
            transcendentals=0,
        ),
        name="mix",
    )(ids, coded, cores)


def lend_kernel(spot_ref, x_ref, *rest, blocks, width):
    count = 1 + max(b[0] for b in blocks)
    weights, out_ref = rest[:count], rest[-1]
    add_ref = rest[count] if len(rest) > count + 1 else None
    spot = spot_ref[0]
    pieces = sum(len(b[2]) for b in blocks)
    piece = x_ref.shape[1] // pieces
    columns = [
        jnp.concatenate(
            [x_ref[:, pl.ds(pl.multiple_of((spot ^ m) * piece, piece), piece)] for m in masks],
            axis=1,
        )
        for _, _, masks in blocks
    ]
    for n in range(0, out_ref.shape[1], width):
        part = slice(n, n + width)
        value = 0.0 if add_ref is None else add_ref[:, part]
        for x, (operand, row, masks) in zip(columns, blocks):
            value = value + dot(x, weights[operand][row : row + piece * len(masks), part])
        out_ref[:, part] = value.astype(out_ref.dtype)


def lend(spot, x, weights, blocks, add, dtype, name):
    rows, depth = x.shape
    columns = weights[0].shape[1]
    whole = pl.BlockSpec(memory_space=pltpu.VMEM)
    operands = (spot.reshape(1), x, *weights) + (() if add is None else (add,))
    return pl.pallas_call(
        functools.partial(lend_kernel, blocks=blocks, width=256),
        out_shape=jax.ShapeDtypeStruct((rows, columns), dtype),
        in_specs=[pl.BlockSpec(memory_space=pltpu.SMEM)] + [whole] * (len(operands) - 1),
        out_specs=whole,
        compiler_params=pltpu.CompilerParams(vmem_limit_bytes=24 * 2**20),
        cost_estimate=pl.CostEstimate(
            flops=2 * rows * depth * columns,
            bytes_accessed=depth * columns * 2 + rows * (depth + columns) * 2,
            transcendentals=0,
        ),
        name=name,
    )(*operands)


def all_cores(cores):
    rep = lax.axis_index("rep")
    core, x = rep % 2, rep // 2
    mate = lax.ppermute(cores, "rep", [(i, i ^ 1) for i in range(4)])
    across = lax.ppermute(cores, "rep", [(i, i ^ 2) for i in range(4)])
    across, mate = lax.optimization_barrier((across, mate))
    corner = lax.ppermute(across, "rep", [(i, i ^ 1) for i in range(4)])
    held = [cores, mate, across, corner]

    def from_rep(r):
        other = rep ^ r
        return lax.select_n(other, *held)

    return jnp.concatenate([from_rep(r) for r in range(4)], axis=0)


IN = [(0, 1), (3, 2)]
OUT = [(1, 0), (2, 3)]
SWAP = [(1, 2), (2, 1)]


def send(x, pairs):
    return lax.ppermute(x, "tp", pairs)


def swap_rep(x, bit):
    return lax.ppermute(x, "rep", [(i, i ^ bit) for i in range(4)])


def swap_groups(x):
    return lax.ppermute(x, "groups", [(0, 1), (1, 0)])


def on_line(activations, row_adapter, base_weight, basis_down, adapter_cores, basis_up):
    me = lax.axis_index("tp")
    inner = (me == 1) | (me == 2)
    left = me < 2
    near_in, far_in = jnp.where(left, 1, 2), jnp.where(left, 2, 1)
    near_out, far_out = jnp.where(left, 0, 3), jnp.where(left, 3, 0)
    spot = lax.axis_index("groups") * 4 + lax.axis_index("rep")
    rows, depth = activations.shape
    piece = depth // 8
    cuts = (0, rows // 2, rows * 3 // 4, rows)
    parts = [slice(a, b) for a, b in zip(cuts, cuts[1:])]

    def weight_of(owner):
        return lax.dynamic_slice_in_dim(base_weight, owner * depth, depth, 0)

    def piece_of(owner):
        return lax.dynamic_slice_in_dim(base_weight, owner * depth + spot * piece, piece, 0)

    swapped = send(activations, SWAP)
    pieces = send(jnp.concatenate([piece_of(far_in), piece_of(far_out)], axis=0), IN)
    cores = all_cores(adapter_cores)
    near, far = pieces[:piece], pieces[piece:]
    partial_value = dot(activations, basis_down)
    top, near, side = lax.optimization_barrier(
        (activations[: rows // 2], near, partial_value.astype(jnp.bfloat16))
    )
    turned = [send(top, IN + OUT)]
    side = send(side, IN).astype(jnp.float32) + partial_value

    near, far, cores, own = lax.optimization_barrier((near, far, cores, activations))
    base = dot(own, weight_of(me))
    near = jnp.concatenate([near, swap_groups(near)], axis=0)
    far = jnp.concatenate([far, swap_rep(far, 2)], axis=0)
    near_more, far_more = swap_rep(near, 2), swap_groups(far)
    near_weights = (near, near_more, swap_rep(near, 1), swap_rep(near_more, 1))
    far_weights = (far, far_more, swap_rep(far, 1), swap_rep(far_more, 1))
    near_blocks = ((0, 0, (0, 4)), (1, 0, (2, 6)), (2, 0, (1, 5)), (3, 0, (3, 7)))
    far_blocks = ((0, 0, (0, 2)), (1, 0, (4, 6)), (2, 0, (1, 3)), (3, 0, (5, 7)))

    bottom, turned[0], swapped, base, half = lax.optimization_barrier(
        (activations[rows // 2 :], turned[0], swapped, base, side.astype(jnp.bfloat16))
    )
    turned.append(send(bottom, IN + OUT))
    coded = (side + send(half, SWAP).astype(jnp.float32)).astype(jnp.bfloat16)
    coded = jnp.where(inner, coded, send(coded, OUT))
    base = base + dot(mix(row_adapter, coded, cores), basis_up)
    base = base + dot(swapped, weight_of(far_in))
    base = base + dot(
        jnp.concatenate(turned, 0), weight_of(jnp.where(inner, near_out, near_in))
    )
    lent = lend(spot, swapped, near_weights, near_blocks, None, jnp.float32, "lend_near")
    last_weight = weight_of(far_out)
    crossed, sent, back, out = [], [], [], []
    for i, p in enumerate(parts):
        x = turned[0] if i == 0 else turned[1][p.start - rows // 2 : p.stop - rows // 2]
        if i == 1:
            x, crossed[0] = lax.optimization_barrier((x, crossed[0]))
        if i > 1:
            x, sent[i - 2] = lax.optimization_barrier((x, sent[i - 2]))
        crossed.append(send(x, SWAP))
        x = crossed[i]
        if i:
            x, back[i - 1] = lax.optimization_barrier((x, back[i - 1]))
        sent.append(lend(spot, x, far_weights, far_blocks, lent[p], jnp.bfloat16, "lend_far"))
        back.append(send(sent[i], OUT))
    for p, x, y in zip(parts, crossed, back):
        out.append((base[p] + dot(x, last_weight) + y.astype(jnp.float32)).astype(jnp.bfloat16))
    return jnp.concatenate(out, axis=0)


def on_any(activations, row_adapter, base_weight, basis_down, adapter_cores, basis_up):
    width = basis_down.shape[1]
    local_count = adapter_cores.shape[0]
    owners = lax.axis_size("rep")
    all_adapters = local_count * owners
    slot_count = all_adapters * BLK
    base = dot(lax.all_gather(activations, "tp", axis=1, tiled=True), base_weight)
    partial_value = dot(activations, basis_down)
    adapter_ids = row_adapter[:, 0]
    onehot = (adapter_ids[:, None] == jnp.arange(all_adapters, dtype=jnp.int32)[None, :]).astype(
        jnp.int32
    )
    earlier = jnp.cumsum(onehot, axis=0) - onehot
    within = jnp.sum(earlier * onehot, axis=1)
    slot_index = adapter_ids * BLK + within
    coded = lax.psum(partial_value, "tp").astype(jnp.bfloat16)
    packed = jnp.zeros((slot_count, width), jnp.bfloat16).at[slot_index].set(coded)
    packed = packed.reshape(owners, local_count, BLK, width)
    mixed_slots = jnp.einsum(
        "nasr,arq->nasq",
        lax.all_to_all(packed, "rep", split_axis=0, concat_axis=0, tiled=True),
        adapter_cores,
        preferred_element_type=jnp.float32,
    ).astype(jnp.bfloat16)
    returned = lax.all_to_all(mixed_slots, "rep", split_axis=0, concat_axis=0, tiled=True).reshape(
        slot_count, width
    )
    mixed = returned[slot_index]
    return (base + dot(mixed, basis_up)).astype(jnp.bfloat16)


def solution(mesh):
    placed = (
        P(("groups", "rep"), "tp"),
        P(("groups", "rep"), None),
        P(None, "tp"),
        P("tp", None),
        P("rep", None, None),
        P(None, "tp"),
    )
    short = (mesh.shape["groups"], mesh.shape["rep"], mesh.shape["tp"]) == (2, 4, 4)
    return jax.shard_map(
        on_line if short else on_any,
        mesh=mesh,
        in_specs=placed,
        out_specs=P(("groups", "rep"), "tp"),
        check_vma=False,
    )
```

```python
import functools

import jax
import jax.numpy as jnp
from jax import lax
from jax.experimental import pallas as pl
from jax.experimental.pallas import tpu as pltpu
from jax.sharding import PartitionSpec as P

BLK = 16


def dot(a, b):
    return jnp.dot(a, b, preferred_element_type=jnp.float32)


def mix_kernel(ids_ref, coded_ref, *rest):
    cores, (mixed_ref, slots_ref) = rest[:-2], rest[-2:]
    rows = coded_ref.shape[0]
    each = cores[0].shape[0]
    adapters = each * len(cores)
    ids = ids_ref[...]
    named = ids == lax.broadcasted_iota(jnp.int32, (rows, adapters), 1)
    below = lax.broadcasted_iota(jnp.int32, (rows, rows), 0) > lax.broadcasted_iota(
        jnp.int32, (rows, rows), 1
    )
    earlier = dot(below.astype(jnp.bfloat16), named.astype(jnp.bfloat16))
    within = jnp.sum(jnp.where(named, earlier, 0.0), axis=1, keepdims=True).astype(jnp.int32)
    slot = ids * BLK + within
    place = (slot == lax.broadcasted_iota(jnp.int32, (rows, adapters * BLK), 1)).astype(
        jnp.bfloat16
    )
    packed = lax.dot_general(
        place, coded_ref[...], (((0,), (0,)), ((), ())), preferred_element_type=jnp.float32
    ).astype(jnp.bfloat16)
    for a in range(adapters):
        slots_ref[a * BLK : (a + 1) * BLK, :] = dot(
            packed[a * BLK : (a + 1) * BLK, :], cores[a // each][a % each]
        ).astype(jnp.bfloat16)
    mixed_ref[...] = dot(place, slots_ref[...]).astype(jnp.bfloat16)


def mix(ids, coded, cores):
    rows, width = coded.shape
    adapters = sum(c.shape[0] for c in cores)
    return pl.pallas_call(
        mix_kernel,
        out_shape=jax.ShapeDtypeStruct((rows, width), jnp.bfloat16),
        scratch_shapes=[pltpu.VMEM((adapters * BLK, width), jnp.bfloat16)],
        compiler_params=pltpu.CompilerParams(vmem_limit_bytes=32 * 2**20),
        cost_estimate=pl.CostEstimate(
            flops=2 * rows * width * (3 * adapters * BLK),
            bytes_accessed=adapters * width * width * 2 + rows * width * 4,
            transcendentals=0,
        ),
        name="mix",
    )(ids, coded, *cores)


def put_beside(out_ref, column, value):
    rows, width = out_ref.shape[0], value.shape[1]
    for b in range(value.shape[0] // rows):
        out_ref[:, column + b * width : column + (b + 1) * width] = value[
            b * rows : (b + 1) * rows
        ]


def pack_kernel(x_ref, value_ref, more_ref, out_ref):
    out_ref[:, : x_ref.shape[1]] = x_ref[...]
    total = value_ref[...] + more_ref[...].astype(jnp.float32)
    put_beside(out_ref, x_ref.shape[1], total.astype(out_ref.dtype))


def pack(x, value, more):
    rows, columns = x.shape
    extra = value.size // rows
    return pl.pallas_call(
        pack_kernel,
        out_shape=jax.ShapeDtypeStruct((rows, columns + extra), x.dtype),
        compiler_params=pltpu.CompilerParams(vmem_limit_bytes=16 * 2**20),
        cost_estimate=pl.CostEstimate(
            flops=value.size, bytes_accessed=4 * rows * (columns + extra), transcendentals=0
        ),
        name="pack",
    )(x, value, more)


def lend_kernel(spot_ref, x_ref, *rest, blocks, width, columns):
    count = 1 + max(b[0] for b in blocks)
    weights, out_ref = rest[:count], rest[-1]
    add_ref = rest[count] if len(rest) > count + 1 else None
    if len(rest) > count + 2:
        put_beside(out_ref, columns, rest[count + 1][...])
    spot = spot_ref[0]
    pieces = sum(len(b[2]) for b in blocks)
    piece = x_ref.shape[1] // pieces
    xs = [
        jnp.concatenate(
            [x_ref[:, pl.ds(pl.multiple_of((spot ^ m) * piece, piece), piece)] for m in masks],
            axis=1,
        )
        for _, _, masks in blocks
    ]
    for n in range(0, columns, width):
        part = slice(n, n + width)
        value = 0.0 if add_ref is None else add_ref[:, part]
        for x, (operand, row, masks) in zip(xs, blocks):
            value = value + dot(x, weights[operand][row : row + piece * len(masks), part])
        out_ref[:, part] = value.astype(out_ref.dtype)


def lend(spot, x, weights, blocks, name, add=None, beside=None, dtype=jnp.bfloat16):
    rows, depth = x.shape
    columns = weights[0].shape[1]
    extra = 0 if beside is None else beside.size // rows
    whole = pl.BlockSpec(memory_space=pltpu.VMEM)
    operands = (spot.reshape(1), x, *weights) + tuple(v for v in (add, beside) if v is not None)
    return pl.pallas_call(
        functools.partial(lend_kernel, blocks=blocks, width=256, columns=columns),
        out_shape=jax.ShapeDtypeStruct((rows, columns + extra), dtype),
        in_specs=[pl.BlockSpec(memory_space=pltpu.SMEM)] + [whole] * (len(operands) - 1),
        out_specs=whole,
        compiler_params=pltpu.CompilerParams(vmem_limit_bytes=24 * 2**20),
        cost_estimate=pl.CostEstimate(
            flops=2 * rows * depth * columns,
            bytes_accessed=depth * columns * 2 + rows * (depth + columns) * 2,
            transcendentals=0,
        ),
        name=name,
    )(*operands)


IN = [(0, 1), (3, 2)]
OUT = [(1, 0), (2, 3)]
SWAP = [(1, 2), (2, 1)]

TURNS = [4, 4]
CROSSINGS = [4, 3, 1]
AFTER = {
    "corner": ("mate", "across"),
    "turn1": ("pieces",),
    "near1": ("across",),
    "far1": ("mate",),
    "own": ("pieces",),
    "near2": ("own",),
    "far2": ("corner",),
    "near4": ("near3",),
    "cross0": ("swap",),
    "cross1": ("own",),
    "cross2": ("lend0",),
    "lend2": ("back0",),
}


def send(x, pairs):
    return lax.ppermute(x, "tp", pairs)


def swap_rep(x, bit):
    return lax.ppermute(x, "rep", [(i, i ^ bit) for i in range(4)])


def swap_groups(x):
    return lax.ppermute(x, "groups", [(0, 1), (1, 0)])


def row_cuts(rows, eighths):
    ends = [0]
    for e in eighths:
        ends.append(ends[-1] + e * rows // 8)
    return list(zip(ends, ends[1:]))


def on_line(activations, row_adapter, base_weight, basis_down, adapter_cores, basis_up):
    me, rep = lax.axis_index("tp"), lax.axis_index("rep")
    inner = (me == 1) | (me == 2)
    left = me < 2
    near_in, far_in = jnp.where(left, 1, 2), jnp.where(left, 2, 1)
    near_out, far_out = jnp.where(left, 0, 3), jnp.where(left, 3, 0)
    spot = lax.axis_index("groups") * 4 + rep
    rows, depth = activations.shape
    width, columns = basis_up.shape
    piece = depth // 8
    turns, crossings = row_cuts(rows, TURNS), row_cuts(rows, CROSSINGS)
    done = {}

    def after(name, value):
        waits = AFTER.get(name, ())
        if not waits:
            return value
        value, held = lax.optimization_barrier((value, [done[w] for w in waits]))
        done.update(zip(waits, held))
        return value

    def move(name, value, how, *args):
        done[name] = how(after(name, value), *args)
        return done[name]

    def weight_of(owner):
        return lax.dynamic_slice_in_dim(base_weight, owner * depth, depth, 0)

    def piece_of(owner):
        return lax.dynamic_slice_in_dim(base_weight, owner * depth + spot * piece, piece, 0)

    def apart(x, start):
        blocks = jnp.split(x[:, start:], (x.shape[1] - start) // width, axis=1)
        return x[:, :start], jnp.concatenate(blocks, axis=0)

    move("swap", activations, send, SWAP)
    partial_value = dot(activations, basis_down)
    pieces = jnp.concatenate([piece_of(far_in), piece_of(far_out)], axis=0)
    pieces = jnp.concatenate([pieces, partial_value.astype(jnp.bfloat16)], axis=1)
    move("pieces", pieces, send, IN)

    move("across", adapter_cores, swap_rep, 2)
    move("mate", adapter_cores, swap_rep, 1)
    move("corner", done["across"], swap_rep, 1)
    each = adapter_cores.shape[0]
    ids = (row_adapter // each ^ rep) * each + row_adapter % each

    def turn(i):
        move(f"turn{i}", activations[slice(*turns[i])], send, IN + OUT)

    def own_dot():
        done["own"] = dot(after("own", activations), weight_of(me))

    turn(0)
    move("near1", done["pieces"][:piece, :columns], swap_groups)
    move("far1", done["pieces"][piece:, :columns], swap_rep, 2)
    turn(1)
    own_dot()
    near = jnp.concatenate([done["pieces"][:piece, :columns], done["near1"]], axis=0)
    far = jnp.concatenate([done["pieces"][piece:, :columns], done["far1"]], axis=0)
    move("near2", near, swap_rep, 2)
    move("far2", far, swap_groups)
    move("near3", near, swap_rep, 1)
    move("far3", far, swap_rep, 1)
    for i in range(2, len(turns)):
        turn(i)
    move("near4", done["near2"], swap_rep, 1)
    move("far4", done["far2"], swap_rep, 1)
    near_blocks = ((0, 0, (0, 4)), (1, 0, (2, 6)), (2, 0, (1, 5)), (3, 0, (3, 7)))
    far_blocks = ((0, 0, (0, 2)), (1, 0, (4, 6)), (2, 0, (1, 3)), (3, 0, (5, 7)))

    def cross(i):
        a, b = crossings[i]
        j = [a >= start and b <= stop for start, stop in turns].index(True)
        x = done[f"turn{j}"][a - turns[j][0] : b - turns[j][0]]
        if i == 0:
            x = pack(x, partial_value, done["pieces"][:, columns:])
        move(f"cross{i}", x, send, SWAP)
        if i == 0:
            done["cross0"], done["side"] = apart(done["cross0"], depth)

    cross(0)
    side = done["pieces"][:, columns:].astype(jnp.float32) + partial_value
    coded = (side + done["side"].astype(jnp.float32)).astype(jnp.bfloat16)
    cross(1)

    done["swap dot"] = dot(after("swap dot", done["swap"]), weight_of(far_in))
    last_weight = weight_of(far_out)
    for i, (a, b) in enumerate(crossings):
        if i == 0:
            weights = (near, done["near2"], done["near3"], done["near4"])
            lent = lend(spot, done["swap"], weights, near_blocks, "lend_near", dtype=jnp.float32)
        x = after(f"lend{i}", done[f"cross{i}"])
        weights = (far, done["far2"], done["far3"], done["far4"])
        done[f"lend{i}"] = lend(
            spot, x, weights, far_blocks, "lend_far", lent[a:b], coded if i == 0 else None
        )
        move(f"back{i}", done[f"lend{i}"], send, OUT)
        if i == 0:
            done["back0"], done["coded"] = apart(done["back0"], columns)
        if i + 2 < len(crossings):
            cross(i + 2)
        if i == 0:
            turned = jnp.concatenate([done[f"turn{j}"] for j in range(len(turns))], 0)
            turned = dot(turned, weight_of(jnp.where(inner, near_out, near_in)))
            base = done["own"] + done["swap dot"] + turned

    cores = (adapter_cores, done["mate"], done["across"], done["corner"])
    mixed = mix(ids, jnp.where(inner, coded, done["coded"]), cores)
    base = base + dot(mixed, basis_up)
    out = []
    for i, (a, b) in enumerate(crossings):
        value = base[a:b] + dot(done[f"cross{i}"], last_weight)
        out.append((value + done[f"back{i}"].astype(jnp.float32)).astype(jnp.bfloat16))
    return jnp.concatenate(out, axis=0)


def on_any(activations, row_adapter, base_weight, basis_down, adapter_cores, basis_up):
    width = basis_down.shape[1]
    local_count = adapter_cores.shape[0]
    owners = lax.axis_size("rep")
    all_adapters = local_count * owners
    slot_count = all_adapters * BLK
    base = dot(lax.all_gather(activations, "tp", axis=1, tiled=True), base_weight)
    partial_value = dot(activations, basis_down)
    adapter_ids = row_adapter[:, 0]
    onehot = (adapter_ids[:, None] == jnp.arange(all_adapters, dtype=jnp.int32)[None, :]).astype(
        jnp.int32
    )
    earlier = jnp.cumsum(onehot, axis=0) - onehot
    within = jnp.sum(earlier * onehot, axis=1)
    slot_index = adapter_ids * BLK + within
    coded = lax.psum(partial_value, "tp").astype(jnp.bfloat16)
    packed = jnp.zeros((slot_count, width), jnp.bfloat16).at[slot_index].set(coded)
    packed = packed.reshape(owners, local_count, BLK, width)
    mixed_slots = jnp.einsum(
        "nasr,arq->nasq",
        lax.all_to_all(packed, "rep", split_axis=0, concat_axis=0, tiled=True),
        adapter_cores,
        preferred_element_type=jnp.float32,
    ).astype(jnp.bfloat16)
    returned = lax.all_to_all(mixed_slots, "rep", split_axis=0, concat_axis=0, tiled=True).reshape(
        slot_count, width
    )
    mixed = returned[slot_index]
    return (base + dot(mixed, basis_up)).astype(jnp.bfloat16)


def solution(mesh):
    placed = (
        P(("groups", "rep"), "tp"),
        P(("groups", "rep"), None),
        P(None, "tp"),
        P("tp", None),
        P("rep", None, None),
        P(None, "tp"),
    )
    short = (mesh.shape["groups"], mesh.shape["rep"], mesh.shape["tp"]) == (2, 4, 4)
    return jax.shard_map(
        on_line if short else on_any,
        mesh=mesh,
        in_specs=placed,
        out_specs=P(("groups", "rep"), "tp"),
        check_vma=False,
    )
```

```python
import functools

import jax
import jax.numpy as jnp
from jax import lax
from jax.experimental import pallas as pl
from jax.experimental.pallas import tpu as pltpu
from jax.sharding import PartitionSpec as P

BLK = 16


def dot(a, b):
    return jnp.dot(a, b, preferred_element_type=jnp.float32)


def mix_kernel(ids_ref, coded_ref, *rest):
    cores, (mixed_ref, slots_ref) = rest[:4], rest[-2:]
    rows = coded_ref.shape[0]
    each = cores[0].shape[0]
    adapters = each * len(cores)
    ids = ids_ref[...]
    named = ids == lax.broadcasted_iota(jnp.int32, (rows, adapters), 1)
    below = lax.broadcasted_iota(jnp.int32, (rows, rows), 0) > lax.broadcasted_iota(
        jnp.int32, (rows, rows), 1
    )
    earlier = dot(below.astype(jnp.bfloat16), named.astype(jnp.bfloat16))
    within = jnp.sum(jnp.where(named, earlier, 0.0), axis=1, keepdims=True).astype(jnp.int32)
    slot = ids * BLK + within
    place = (slot == lax.broadcasted_iota(jnp.int32, (rows, adapters * BLK), 1)).astype(
        jnp.bfloat16
    )
    packed = lax.dot_general(
        place, coded_ref[...], (((0,), (0,)), ((), ())), preferred_element_type=jnp.float32
    ).astype(jnp.bfloat16)
    for a in range(adapters):
        slots_ref[a * BLK : (a + 1) * BLK, :] = dot(
            packed[a * BLK : (a + 1) * BLK, :], cores[a // each][a % each]
        ).astype(jnp.bfloat16)
    mixed_ref[...] = dot(place, slots_ref[...]).astype(jnp.bfloat16)


def mix(ids, coded, cores, waits):
    rows, width = coded.shape
    adapters = sum(c.shape[0] for c in cores)
    return pl.pallas_call(
        mix_kernel,
        out_shape=jax.ShapeDtypeStruct((rows, width), jnp.bfloat16),
        in_specs=[pl.BlockSpec(memory_space=pltpu.VMEM)] * (2 + len(cores))
        + [pl.BlockSpec(memory_space=pl.ANY)] * len(waits),
        scratch_shapes=[pltpu.VMEM((adapters * BLK, width), jnp.bfloat16)],
        compiler_params=pltpu.CompilerParams(vmem_limit_bytes=10 * 2**20),
        cost_estimate=pl.CostEstimate(
            flops=2 * rows * width * (3 * adapters * BLK),
            bytes_accessed=adapters * width * width * 2 + rows * width * 4,
            transcendentals=0,
        ),
        name="mix",
    )(ids, coded, *cores, *waits)


def pick_kernel(which_ref, x_ref, beside_ref, out_ref):
    columns = x_ref.shape[1]
    out_ref[:, :columns] = x_ref[...]
    out_ref[:, columns:] = beside_ref[...]


def pick(x, blocks, rows, beside):
    columns, more = x.shape[1], beside.shape[1]
    return pl.pallas_call(
        pick_kernel,
        out_shape=jax.ShapeDtypeStruct((blocks.size * rows, columns + more), x.dtype),
        grid_spec=pltpu.PrefetchScalarGridSpec(
            num_scalar_prefetch=1,
            grid=(blocks.size,),
            in_specs=[
                pl.BlockSpec((rows, columns), lambda i, which: (which[i], 0)),
                pl.BlockSpec((rows, more), lambda i, which: (i, 0)),
            ],
            out_specs=pl.BlockSpec((rows, columns + more), lambda i, which: (i, 0)),
        ),
        cost_estimate=pl.CostEstimate(
            flops=0, bytes_accessed=4 * blocks.size * rows * columns, transcendentals=0
        ),
        name="pick",
    )(blocks, x, beside)


def lend_kernel(spot_ref, *refs, count, blocks, width, added):
    xs, rest = refs[:count], refs[count:]
    out_ref = rest[-1]
    piece = xs[0].shape[1] // sum(len(masks) for _, masks in blocks)
    spot = spot_ref[0]
    start = 0
    for x_ref in xs:
        rows = slice(start, start + x_ref.shape[0])
        start = rows.stop
        columns = [
            jnp.concatenate(
                [x_ref[:, pl.ds(pl.multiple_of((spot ^ m) * piece, piece), piece)] for m in masks],
                axis=1,
            )
            for _, masks in blocks
        ]
        for n in range(0, out_ref.shape[1], width):
            part = slice(n, n + width)
            value = rest[len(blocks)][rows, part] if added else 0.0
            for x, (operand, _) in zip(columns, blocks):
                value = value + dot(x, rest[operand][:, part])
            out_ref[rows, part] = value.astype(out_ref.dtype)


def lend(spot, xs, weights, masks, name, add=None, waits=(), dtype=jnp.bfloat16):
    rows, depth = sum(x.shape[0] for x in xs), xs[0].shape[1]
    columns = weights[0].shape[1]
    whole = pl.BlockSpec(memory_space=pltpu.VMEM)
    operands = (*xs, *weights, *(() if add is None else (add,)))
    return pl.pallas_call(
        functools.partial(
            lend_kernel,
            count=len(xs),
            blocks=tuple(enumerate(masks)),
            width=256,
            added=add is not None,
        ),
        out_shape=jax.ShapeDtypeStruct((rows, columns), dtype),
        in_specs=[pl.BlockSpec(memory_space=pltpu.SMEM)]
        + [whole] * len(operands)
        + [pl.BlockSpec(memory_space=pl.ANY)] * len(waits),
        out_specs=whole,
        compiler_params=pltpu.CompilerParams(vmem_limit_bytes=12 * 2**20),
        cost_estimate=pl.CostEstimate(
            flops=2 * rows * depth * columns,
            bytes_accessed=depth * columns * 2 + rows * (depth + columns) * 2,
            transcendentals=0,
        ),
        name=name,
    )(spot.reshape(1), *operands, *waits)


IN = [(0, 1), (3, 2)]
OUT = [(1, 0), (2, 3)]
SWAP = [(1, 2), (2, 1)]

TURNS = (3, 3, 2)
CROSSINGS = (3, 3, 1, 1)
LENDS = (2, 2)
AFTER = {
    "corner": ("mate", "own"),
    "near1": ("corner",),
    "far1": ("corner",),
    "near2": ("far3",),
    "far2": ("far3",),
    "turn1": ("turn0", "swap", "half", "near1", "far1"),
    "turn2": ("turn1", "cross0", "far3"),
    "near4": ("coded", "cross0", "turn1", "turn2"),
    "far4": ("coded", "cross0", "turn2"),
    "lend0": ("turn2",),
    "lend1": ("base", "cross2"),
    "mix": ("lent",),
    "lent": ("far4",),
    "near3": ("coded",),
}


def send(x, pairs):
    return lax.ppermute(x, "tp", pairs)


def swap_rep(x, bit):
    return lax.ppermute(x, "rep", [(i, i ^ bit) for i in range(4)])


def swap_groups(x):
    return lax.ppermute(x, "groups", [(0, 1), (1, 0)])


def row_cuts(rows, eighths):
    ends = [0]
    for e in eighths:
        ends.append(ends[-1] + e * rows // 8)
    return list(zip(ends, ends[1:]))


def on_line(activations, row_adapter, base_weight, basis_down, adapter_cores, basis_up):
    me, rep = lax.axis_index("tp"), lax.axis_index("rep")
    inner = (me == 1) | (me == 2)
    left = me < 2
    near_in, far_in = jnp.where(left, 1, 2), jnp.where(left, 2, 1)
    near_out, far_out = jnp.where(left, 0, 3), jnp.where(left, 3, 0)
    spot = lax.axis_index("groups") * 4 + rep
    rows, depth = activations.shape
    piece = depth // 8
    turns, crossings = row_cuts(rows, TURNS), row_cuts(rows, CROSSINGS)
    done = {}

    def after(name, value):
        waits = AFTER.get(name, ())
        if not waits:
            return value
        value, held = lax.optimization_barrier((value, [done[w] for w in waits]))
        done.update(zip(waits, held))
        return value

    def held(name):
        return [done[w] for w in AFTER.get(name, ())]

    def move(name, value, how, *args):
        done[name] = how(after(name, value), *args)
        return done[name]

    def weight_of(owner):
        return lax.dynamic_slice_in_dim(base_weight, owner * depth, depth, 0)

    move("swap", activations, send, SWAP)
    eighths = jnp.stack([far_in * 8 + spot, far_out * 8 + spot]).astype(jnp.int32)
    partial_value = dot(activations, basis_down)
    pieces = pick(base_weight, eighths, piece, partial_value.astype(jnp.bfloat16))
    move("pieces", pieces, send, IN)
    columns = base_weight.shape[1]

    move("across", adapter_cores, swap_rep, 2)
    move("mate", adapter_cores, swap_rep, 1)
    done["own"] = dot(after("own", activations), weight_of(me))
    move("corner", done["across"], swap_rep, 1)
    each = adapter_cores.shape[0]
    ids = (row_adapter // each ^ rep) * each + row_adapter % each

    def turn(i):
        move(f"turn{i}", activations[slice(*turns[i])], send, IN + OUT)

    def turned(a, b):
        j = [a >= start and b <= stop for start, stop in turns].index(True)
        return done[f"turn{j}"][a - turns[j][0] : b - turns[j][0]]

    def cross(i):
        move(f"cross{i}", turned(*crossings[i]), send, SWAP)

    turn(0)
    side = done["pieces"][:, columns:].astype(jnp.float32) + partial_value
    move("half", side.astype(jnp.bfloat16), send, SWAP)
    move("near1", done["pieces"][:piece, :columns], swap_groups)
    move("far1", done["pieces"][piece:, :columns], swap_rep, 2)
    turn(1)
    done["swap dot"] = done["own"] + dot(after("swap dot", done["swap"]), weight_of(far_in))
    coded = (side + done["half"].astype(jnp.float32)).astype(jnp.bfloat16)
    move("coded", coded, send, OUT)
    near = jnp.concatenate([done["pieces"][:piece, :columns], done["near1"]], axis=0)
    far = jnp.concatenate([done["pieces"][piece:, :columns], done["far1"]], axis=0)
    move("near3", near, swap_rep, 1)
    move("far3", far, swap_rep, 1)
    move("near2", near, swap_rep, 2)
    move("far2", far, swap_groups)
    cross(0)
    for i in range(2, len(turns)):
        turn(i)
    near_masks, far_masks = ((0, 4), (2, 6), (1, 5), (3, 7)), ((0, 2), (4, 6), (1, 3), (5, 7))

    for i in range(1, len(crossings)):
        cross(i)
    move("near4", done["near2"], swap_rep, 1)
    move("far4", done["far2"], swap_rep, 1)

    weights = (near, done["near2"], done["near3"], done["near4"])
    done["lent"] = lend(
        spot, [done["swap"]], weights, near_masks, "lend_near", None, held("lent"), jnp.float32
    )
    weights = (far, done["far2"], done["far3"], done["far4"])
    first = 0
    for i, count in enumerate(LENDS):
        chunks = range(first, first + count)
        first += count
        xs, add = [done[f"cross{j}"] for j in chunks], done["lent"]
        add = add[crossings[chunks[0]][0] : crossings[chunks[-1]][1]]
        done[f"lend{i}"] = lend(spot, xs, weights, far_masks, "lend_far", add, held(f"lend{i}"))
        move(f"back{i}", done[f"lend{i}"], send, OUT)
        if i == 0:
            cores = (adapter_cores, done["mate"], done["across"], done["corner"])
            mixed = mix(ids, jnp.where(inner, coded, done["coded"]), cores, held("mix"))
            done["base"] = done["swap dot"] + dot(mixed, basis_up)

    last_weight = weight_of(far_out)
    turned_weight = weight_of(jnp.where(inner, near_out, near_in))
    back = [done[f"back{i}"] for i in range(len(LENDS))]
    out = []
    first = 0
    for i, count in enumerate(LENDS):
        start = crossings[first][0]
        for a, b in crossings[first : first + count]:
            value = done["base"][a:b] + dot(turned(a, b), turned_weight)
            value = value + dot(done[f"cross{len(out)}"], last_weight)
            value = value + back[i][a - start : b - start].astype(jnp.float32)
            out.append(value.astype(jnp.bfloat16))
        first += count
    return jnp.concatenate(out, axis=0)


def on_any(activations, row_adapter, base_weight, basis_down, adapter_cores, basis_up):
    width = basis_down.shape[1]
    local_count = adapter_cores.shape[0]
    owners = lax.axis_size("rep")
    all_adapters = local_count * owners
    slot_count = all_adapters * BLK
    base = dot(lax.all_gather(activations, "tp", axis=1, tiled=True), base_weight)
    partial_value = dot(activations, basis_down)
    adapter_ids = row_adapter[:, 0]
    onehot = (adapter_ids[:, None] == jnp.arange(all_adapters, dtype=jnp.int32)[None, :]).astype(
        jnp.int32
    )
    earlier = jnp.cumsum(onehot, axis=0) - onehot
    within = jnp.sum(earlier * onehot, axis=1)
    slot_index = adapter_ids * BLK + within
    coded = lax.psum(partial_value, "tp").astype(jnp.bfloat16)
    packed = jnp.zeros((slot_count, width), jnp.bfloat16).at[slot_index].set(coded)
    packed = packed.reshape(owners, local_count, BLK, width)
    mixed_slots = jnp.einsum(
        "nasr,arq->nasq",
        lax.all_to_all(packed, "rep", split_axis=0, concat_axis=0, tiled=True),
        adapter_cores,
        preferred_element_type=jnp.float32,
    ).astype(jnp.bfloat16)
    returned = lax.all_to_all(mixed_slots, "rep", split_axis=0, concat_axis=0, tiled=True).reshape(
        slot_count, width
    )
    mixed = returned[slot_index]
    return (base + dot(mixed, basis_up)).astype(jnp.bfloat16)


def solution(mesh):
    placed = (
        P(("groups", "rep"), "tp"),
        P(("groups", "rep"), None),
        P(None, "tp"),
        P("tp", None),
        P("rep", None, None),
        P(None, "tp"),
    )
    short = (mesh.shape["groups"], mesh.shape["rep"], mesh.shape["tp"]) == (2, 4, 4)
    return jax.shard_map(
        on_line if short else on_any,
        mesh=mesh,
        in_specs=placed,
        out_specs=P(("groups", "rep"), "tp"),
        check_vma=False,
    )
```

```python
import functools

import jax
import jax.numpy as jnp
from jax import lax
from jax.experimental import pallas as pl
from jax.experimental.pallas import tpu as pltpu
from jax.sharding import PartitionSpec as P

BLK = 16


def dot(a, b):
    return jnp.dot(a, b, preferred_element_type=jnp.float32)


def mix_kernel(ids_ref, coded_ref, *rest):
    cores, (mixed_ref, slots_ref) = rest[:4], rest[-2:]
    rows = coded_ref.shape[0]
    each = cores[0].shape[0]
    adapters = each * len(cores)
    ids = ids_ref[...]
    named = ids == lax.broadcasted_iota(jnp.int32, (rows, adapters), 1)
    below = lax.broadcasted_iota(jnp.int32, (rows, rows), 0) > lax.broadcasted_iota(
        jnp.int32, (rows, rows), 1
    )
    earlier = dot(below.astype(jnp.bfloat16), named.astype(jnp.bfloat16))
    within = jnp.sum(jnp.where(named, earlier, 0.0), axis=1, keepdims=True).astype(jnp.int32)
    slot = ids * BLK + within
    place = (slot == lax.broadcasted_iota(jnp.int32, (rows, adapters * BLK), 1)).astype(
        jnp.bfloat16
    )
    packed = lax.dot_general(
        place, coded_ref[...], (((0,), (0,)), ((), ())), preferred_element_type=jnp.float32
    ).astype(jnp.bfloat16)
    for a in range(adapters):
        slots_ref[a * BLK : (a + 1) * BLK, :] = dot(
            packed[a * BLK : (a + 1) * BLK, :], cores[a // each][a % each]
        ).astype(jnp.bfloat16)
    mixed_ref[...] = dot(place, slots_ref[...]).astype(jnp.bfloat16)


def mix(ids, coded, cores, waits):
    rows, width = coded.shape
    adapters = sum(c.shape[0] for c in cores)
    return pl.pallas_call(
        mix_kernel,
        out_shape=jax.ShapeDtypeStruct((rows, width), jnp.bfloat16),
        in_specs=[pl.BlockSpec(memory_space=pltpu.VMEM)] * (2 + len(cores))
        + [pl.BlockSpec(memory_space=pl.ANY)] * len(waits),
        scratch_shapes=[pltpu.VMEM((adapters * BLK, width), jnp.bfloat16)],
        compiler_params=pltpu.CompilerParams(vmem_limit_bytes=10 * 2**20),
        cost_estimate=pl.CostEstimate(
            flops=2 * rows * width * (3 * adapters * BLK),
            bytes_accessed=adapters * width * width * 2 + rows * width * 4,
            transcendentals=0,
        ),
        name="mix",
    )(ids, coded, *cores, *waits)


def pick_kernel(which_ref, x_ref, out_ref):
    out_ref[...] = x_ref[...]


def pick(x, blocks, rows):
    columns = x.shape[1]
    return pl.pallas_call(
        pick_kernel,
        out_shape=jax.ShapeDtypeStruct((blocks.size * rows, columns), x.dtype),
        grid_spec=pltpu.PrefetchScalarGridSpec(
            num_scalar_prefetch=1,
            grid=(blocks.size,),
            in_specs=[pl.BlockSpec((rows, columns), lambda i, which: (which[i], 0))],
            out_specs=pl.BlockSpec((rows, columns), lambda i, which: (i, 0)),
        ),
        cost_estimate=pl.CostEstimate(
            flops=0, bytes_accessed=4 * blocks.size * rows * columns, transcendentals=0
        ),
        name="pick",
    )(blocks, x)


def lend_kernel(spot_ref, *refs, count, blocks, width, added):
    xs, rest = refs[:count], refs[count:]
    out_ref = rest[-1]
    piece = xs[0].shape[1] // sum(len(masks) for _, masks in blocks)
    spot = spot_ref[0]
    start = 0
    for x_ref in xs:
        rows = slice(start, start + x_ref.shape[0])
        start = rows.stop
        columns = [
            jnp.concatenate(
                [x_ref[:, pl.ds(pl.multiple_of((spot ^ m) * piece, piece), piece)] for m in masks],
                axis=1,
            )
            for _, masks in blocks
        ]
        for n in range(0, out_ref.shape[1], width):
            part = slice(n, n + width)
            value = rest[len(blocks)][rows, part] if added else 0.0
            for x, (operand, _) in zip(columns, blocks):
                value = value + dot(x, rest[operand][:, part])
            out_ref[rows, part] = value.astype(out_ref.dtype)


def lend(spot, xs, weights, masks, name, add=None, waits=(), dtype=jnp.bfloat16):
    rows, depth = sum(x.shape[0] for x in xs), xs[0].shape[1]
    columns = weights[0].shape[1]
    whole = pl.BlockSpec(memory_space=pltpu.VMEM)
    operands = (*xs, *weights, *(() if add is None else (add,)))
    return pl.pallas_call(
        functools.partial(
            lend_kernel,
            count=len(xs),
            blocks=tuple(enumerate(masks)),
            width=256,
            added=add is not None,
        ),
        out_shape=jax.ShapeDtypeStruct((rows, columns), dtype),
        in_specs=[pl.BlockSpec(memory_space=pltpu.SMEM)]
        + [whole] * len(operands)
        + [pl.BlockSpec(memory_space=pl.ANY)] * len(waits),
        out_specs=whole,
        compiler_params=pltpu.CompilerParams(vmem_limit_bytes=12 * 2**20),
        cost_estimate=pl.CostEstimate(
            flops=2 * rows * depth * columns,
            bytes_accessed=depth * columns * 2 + rows * (depth + columns) * 2,
            transcendentals=0,
        ),
        name=name,
    )(spot.reshape(1), *operands, *waits)


IN = [(0, 1), (3, 2)]
OUT = [(1, 0), (2, 3)]
SWAP = [(1, 2), (2, 1)]

TURNS = (4, 2, 2)
CROSSINGS = (4, 2, 2)
LENDS = (1, 1, 1)
RIDE = 1
AFTER = {
    "corner": ("mate", "own"),
    "near1": ("corner",),
    "far1": ("corner",),
    "near2": ("near3", "far3"),
    "far2": ("near3", "far3"),
    "turn1": ("turn0", "near1", "far1"),
    "turn2": ("turn1",),
    "cross0": ("swap",),
    "near4": ("cross0",),
    "far4": ("cross0",),
    "lend1": ("lend0",),
    "lend2": ("lend1",),
    "mix": ("lend1",),
    "lent": ("far4",),
    "half": ("swap dot",),
    "turned": ("lend2",),
    "cross2": ("lend0",),
}


def send(x, pairs):
    return lax.ppermute(x, "tp", pairs)


def swap_rep(x, bit):
    return lax.ppermute(x, "rep", [(i, i ^ bit) for i in range(4)])


def swap_groups(x):
    return lax.ppermute(x, "groups", [(0, 1), (1, 0)])


def row_cuts(rows, eighths):
    ends = [0]
    for e in eighths:
        ends.append(ends[-1] + e * rows // 8)
    return list(zip(ends, ends[1:]))


def on_line(activations, row_adapter, base_weight, basis_down, adapter_cores, basis_up):
    me, rep = lax.axis_index("tp"), lax.axis_index("rep")
    inner = (me == 1) | (me == 2)
    left = me < 2
    near_in, far_in = jnp.where(left, 1, 2), jnp.where(left, 2, 1)
    near_out, far_out = jnp.where(left, 0, 3), jnp.where(left, 3, 0)
    spot = lax.axis_index("groups") * 4 + rep
    rows, depth = activations.shape
    width = basis_up.shape[0]
    piece = depth // 8
    turns, crossings = row_cuts(rows, TURNS), row_cuts(rows, CROSSINGS)
    done = {}

    def after(name, value):
        waits = AFTER.get(name, ())
        if not waits:
            return value
        value, held = lax.optimization_barrier((value, [done[w] for w in waits]))
        done.update(zip(waits, held))
        return value

    def held(name):
        return [done[w] for w in AFTER.get(name, ())]

    def move(name, value, how, *args):
        done[name] = how(after(name, value), *args)
        return done[name]

    def weight_of(owner):
        return lax.dynamic_slice_in_dim(base_weight, owner * depth, depth, 0)

    move("swap", activations, send, SWAP)
    eighths = jnp.stack([far_in * 8 + spot, far_out * 8 + spot]).astype(jnp.int32)
    move("pieces", pick(base_weight, eighths, piece), send, IN)
    partial_value = dot(activations, basis_down)

    move("across", adapter_cores, swap_rep, 2)
    move("mate", adapter_cores, swap_rep, 1)
    done["own"] = dot(after("own", activations), weight_of(me))
    move("corner", done["across"], swap_rep, 1)
    each = adapter_cores.shape[0]
    ids = (row_adapter // each ^ rep) * each + row_adapter % each

    def turn(i):
        x = activations[slice(*turns[i])]
        if i == RIDE:
            blocks = partial_value.astype(jnp.bfloat16).reshape(-1, *x.shape[:1], width)
            x = jnp.concatenate([x, *blocks], axis=1)
        move(f"turn{i}", x, send, IN + OUT)
        if i == RIDE:
            x = done[f"turn{i}"]
            blocks = jnp.split(x[:, depth:], (x.shape[1] - depth) // width, axis=1)
            done[f"turn{i}"], done["part"] = x[:, :depth], jnp.concatenate(blocks, axis=0)

    def turned(a, b):
        j = [a >= start and b <= stop for start, stop in turns].index(True)
        return done[f"turn{j}"][a - turns[j][0] : b - turns[j][0]]

    def cross(i):
        move(f"cross{i}", turned(*crossings[i]), send, SWAP)

    turn(0)
    move("near1", done["pieces"][:piece], swap_groups)
    move("far1", done["pieces"][piece:], swap_rep, 2)
    turn(1)
    done["swap dot"] = done["own"] + dot(after("swap dot", done["swap"]), weight_of(far_in))
    near = jnp.concatenate([done["pieces"][:piece], done["near1"]], axis=0)
    far = jnp.concatenate([done["pieces"][piece:], done["far1"]], axis=0)
    move("near3", near, swap_rep, 1)
    move("far3", far, swap_rep, 1)
    move("near2", near, swap_rep, 2)
    move("far2", far, swap_groups)
    cross(0)
    for i in range(2, len(turns)):
        turn(i)
    near_masks, far_masks = ((0, 4), (2, 6), (1, 5), (3, 7)), ((0, 2), (4, 6), (1, 3), (5, 7))

    cross(1)
    side = done["part"].astype(jnp.float32) + partial_value
    move("half", side.astype(jnp.bfloat16), send, SWAP)
    coded = (side + done["half"].astype(jnp.float32)).astype(jnp.bfloat16)
    move("coded", coded, send, OUT)
    move("near4", done["near2"], swap_rep, 1)
    move("far4", done["far2"], swap_rep, 1)

    weights = (near, done["near2"], done["near3"], done["near4"])
    done["lent"] = lend(
        spot, [done["swap"]], weights, near_masks, "lend_near", None, held("lent"), jnp.float32
    )
    weights = (far, done["far2"], done["far3"], done["far4"])
    first = 0
    for i, count in enumerate(LENDS):
        chunks = range(first, first + count)
        first += count
        if i == len(LENDS) - 1:
            cores = (adapter_cores, done["mate"], done["across"], done["corner"])
            mixed = mix(ids, jnp.where(inner, coded, done["coded"]), cores, held("mix"))
            done["base"] = done["swap dot"] + dot(mixed, basis_up)
        xs, add = [done[f"cross{j}"] for j in chunks], done["lent"]
        add = add[crossings[chunks[0]][0] : crossings[chunks[-1]][1]]
        done[f"lend{i}"] = lend(spot, xs, weights, far_masks, "lend_far", add, held(f"lend{i}"))
        for j in range(2, len(crossings)) if i == 0 else ():
            cross(j)
        if i == len(LENDS) - 1:
            x = jnp.concatenate([done[f"turn{j}"] for j in range(len(turns))], axis=0)
            owner = jnp.where(inner, near_out, near_in)
            last = done["base"] + dot(after("turned", x), weight_of(owner))
        move(f"back{i}", done[f"lend{i}"], send, OUT)

    last_weight = weight_of(far_out)
    back = [done[f"back{i}"] for i in range(len(LENDS))]
    out = []
    first = 0
    for i, count in enumerate(LENDS):
        start = crossings[first][0]
        for a, b in crossings[first : first + count]:
            value = last[a:b] + dot(done[f"cross{len(out)}"], last_weight)
            value = value + back[i][a - start : b - start].astype(jnp.float32)
            out.append(value.astype(jnp.bfloat16))
        first += count
    return jnp.concatenate(out, axis=0)


def on_any(activations, row_adapter, base_weight, basis_down, adapter_cores, basis_up):
    width = basis_down.shape[1]
    local_count = adapter_cores.shape[0]
    owners = lax.axis_size("rep")
    all_adapters = local_count * owners
    slot_count = all_adapters * BLK
    base = dot(lax.all_gather(activations, "tp", axis=1, tiled=True), base_weight)
    partial_value = dot(activations, basis_down)
    adapter_ids = row_adapter[:, 0]
    onehot = (adapter_ids[:, None] == jnp.arange(all_adapters, dtype=jnp.int32)[None, :]).astype(
        jnp.int32
    )
    earlier = jnp.cumsum(onehot, axis=0) - onehot
    within = jnp.sum(earlier * onehot, axis=1)
    slot_index = adapter_ids * BLK + within
    coded = lax.psum(partial_value, "tp").astype(jnp.bfloat16)
    packed = jnp.zeros((slot_count, width), jnp.bfloat16).at[slot_index].set(coded)
    packed = packed.reshape(owners, local_count, BLK, width)
    mixed_slots = jnp.einsum(
        "nasr,arq->nasq",
        lax.all_to_all(packed, "rep", split_axis=0, concat_axis=0, tiled=True),
        adapter_cores,
        preferred_element_type=jnp.float32,
    ).astype(jnp.bfloat16)
    returned = lax.all_to_all(mixed_slots, "rep", split_axis=0, concat_axis=0, tiled=True).reshape(
        slot_count, width
    )
    mixed = returned[slot_index]
    return (base + dot(mixed, basis_up)).astype(jnp.bfloat16)


def solution(mesh):
    placed = (
        P(("groups", "rep"), "tp"),
        P(("groups", "rep"), None),
        P(None, "tp"),
        P("tp", None),
        P("rep", None, None),
        P(None, "tp"),
    )
    short = (mesh.shape["groups"], mesh.shape["rep"], mesh.shape["tp"]) == (2, 4, 4)
    return jax.shard_map(
        on_line if short else on_any,
        mesh=mesh,
        in_specs=placed,
        out_specs=P(("groups", "rep"), "tp"),
        check_vma=False,
    )
```

```python
import functools

import jax
import jax.numpy as jnp
from jax import lax
from jax.experimental import pallas as pl
from jax.experimental.pallas import tpu as pltpu
from jax.sharding import PartitionSpec as P

BLK = 16


def dot(a, b):
    return jnp.dot(a, b, preferred_element_type=jnp.float32)


def mix_kernel(rep_ref, ids_ref, coded_ref, *rest):
    cores, (mixed_ref, slots_ref) = rest[:4], rest[-2:]
    rows = coded_ref.shape[0]
    each = cores[0].shape[0]
    adapters = each * len(cores)
    ids = ids_ref[...] ^ (rep_ref[0] * each)
    named = ids == lax.broadcasted_iota(jnp.int32, (rows, adapters), 1)
    below = lax.broadcasted_iota(jnp.int32, (rows, rows), 0) > lax.broadcasted_iota(
        jnp.int32, (rows, rows), 1
    )
    earlier = dot(below.astype(jnp.bfloat16), named.astype(jnp.bfloat16))
    within = jnp.sum(jnp.where(named, earlier, 0.0), axis=1, keepdims=True).astype(jnp.int32)
    slot = ids * BLK + within
    place = (slot == lax.broadcasted_iota(jnp.int32, (rows, adapters * BLK), 1)).astype(
        jnp.bfloat16
    )
    packed = lax.dot_general(
        place, coded_ref[...], (((0,), (0,)), ((), ())), preferred_element_type=jnp.float32
    ).astype(jnp.bfloat16)
    for a in range(adapters):
        slots_ref[a * BLK : (a + 1) * BLK, :] = dot(
            packed[a * BLK : (a + 1) * BLK, :], cores[a // each][a % each]
        ).astype(jnp.bfloat16)
    mixed_ref[...] = dot(place, slots_ref[...]).astype(jnp.bfloat16)


def mix(rep, ids, coded, cores, waits):
    rows, width = coded.shape
    adapters = sum(c.shape[0] for c in cores)
    return pl.pallas_call(
        mix_kernel,
        out_shape=jax.ShapeDtypeStruct((rows, width), jnp.bfloat16),
        in_specs=[pl.BlockSpec(memory_space=pltpu.SMEM)]
        + [pl.BlockSpec(memory_space=pltpu.VMEM)] * (2 + len(cores))
        + [pl.BlockSpec(memory_space=pl.ANY)] * len(waits),
        scratch_shapes=[pltpu.VMEM((adapters * BLK, width), jnp.bfloat16)],
        compiler_params=pltpu.CompilerParams(vmem_limit_bytes=10 * 2**20),
        cost_estimate=pl.CostEstimate(
            flops=2 * rows * width * (3 * adapters * BLK),
            bytes_accessed=adapters * width * width * 2 + rows * width * 4,
            transcendentals=0,
        ),
        name="mix",
    )(rep.reshape(1), ids, coded, *cores, *waits)


def pick_kernel(which_ref, x_ref, out_ref):
    out_ref[...] = x_ref[...]


def pick(x, blocks, rows):
    columns = x.shape[1]
    return pl.pallas_call(
        pick_kernel,
        out_shape=jax.ShapeDtypeStruct((blocks.size * rows, columns), x.dtype),
        grid_spec=pltpu.PrefetchScalarGridSpec(
            num_scalar_prefetch=1,
            grid=(blocks.size,),
            in_specs=[pl.BlockSpec((rows, columns), lambda i, which: (which[i], 0))],
            out_specs=pl.BlockSpec((rows, columns), lambda i, which: (i, 0)),
        ),
        cost_estimate=pl.CostEstimate(
            flops=0, bytes_accessed=4 * blocks.size * rows * columns, transcendentals=0
        ),
        name="pick",
    )(blocks, x)


def lend_kernel(spot_ref, *refs, count, blocks, width, added):
    xs, rest = refs[:count], refs[count:]
    out_ref = rest[-1]
    piece = xs[0].shape[1] // sum(len(masks) for _, masks in blocks)
    spot = spot_ref[0]
    start = 0
    for x_ref in xs:
        rows = slice(start, start + x_ref.shape[0])
        start = rows.stop
        columns = [
            jnp.concatenate(
                [x_ref[:, pl.ds(pl.multiple_of((spot ^ m) * piece, piece), piece)] for m in masks],
                axis=1,
            )
            for _, masks in blocks
        ]
        for n in range(0, out_ref.shape[1], width):
            part = slice(n, n + width)
            value = rest[len(blocks)][rows, part] if added else 0.0
            for x, (operand, _) in zip(columns, blocks):
                value = value + dot(x, rest[operand][:, part])
            out_ref[rows, part] = value.astype(out_ref.dtype)


def lend(spot, xs, weights, masks, name, add=None, waits=(), dtype=jnp.bfloat16):
    rows, depth = sum(x.shape[0] for x in xs), xs[0].shape[1]
    columns = weights[0].shape[1]
    whole = pl.BlockSpec(memory_space=pltpu.VMEM)
    operands = (*xs, *weights, *(() if add is None else (add,)))
    return pl.pallas_call(
        functools.partial(
            lend_kernel,
            count=len(xs),
            blocks=tuple(enumerate(masks)),
            width=256,
            added=add is not None,
        ),
        out_shape=jax.ShapeDtypeStruct((rows, columns), dtype),
        in_specs=[pl.BlockSpec(memory_space=pltpu.SMEM)]
        + [whole] * len(operands)
        + [pl.BlockSpec(memory_space=pl.ANY)] * len(waits),
        out_specs=whole,
        compiler_params=pltpu.CompilerParams(vmem_limit_bytes=12 * 2**20),
        cost_estimate=pl.CostEstimate(
            flops=2 * rows * depth * columns,
            bytes_accessed=depth * columns * 2 + rows * (depth + columns) * 2,
            transcendentals=0,
        ),
        name=name,
    )(spot.reshape(1), *operands, *waits)


IN = [(0, 1), (3, 2)]
OUT = [(1, 0), (2, 3)]
SWAP = [(1, 2), (2, 1)]

TURNS = (4, 2, 2)
CROSSINGS = (4, 2, 2)
LENDS = (1, 1, 1)
RIDE = 1
AFTER = {
    "corner": ("mate", "own"),
    "near1": ("corner",),
    "far1": ("corner",),
    "near2": ("near3", "far3"),
    "far2": ("far3",),
    "turn1": ("far1",),
    "turn2": ("turn1",),
    "cross0": ("far1", "near1"),
    "near4": ("cross0", "turn1"),
    "far4": ("cross0", "turn1"),
    "lend1": ("lend0", "back0"),
    "lend2": ("lend1",),
    "mix": ("lend0",),
    "lent": ("far4",),
    "half": ("lent", "cross0"),
    "turned": ("lend2",),
    "cross2": ("lend0",),
    "swap dot": ("turn0",),
    "cross1": ("cross0",),
}


def send(x, pairs):
    return lax.ppermute(x, "tp", pairs)


def swap_rep(x, bit):
    return lax.ppermute(x, "rep", [(i, i ^ bit) for i in range(4)])


def swap_groups(x):
    return lax.ppermute(x, "groups", [(0, 1), (1, 0)])


def row_cuts(rows, eighths):
    ends = [0]
    for e in eighths:
        ends.append(ends[-1] + e * rows // 8)
    return list(zip(ends, ends[1:]))


def on_line(activations, row_adapter, base_weight, basis_down, adapter_cores, basis_up):
    me, rep = lax.axis_index("tp"), lax.axis_index("rep")
    inner = (me == 1) | (me == 2)
    left = me < 2
    near_in, far_in = jnp.where(left, 1, 2), jnp.where(left, 2, 1)
    near_out, far_out = jnp.where(left, 0, 3), jnp.where(left, 3, 0)
    spot = lax.axis_index("groups") * 4 + rep
    rows, depth = activations.shape
    width = basis_up.shape[0]
    piece = depth // 8
    turns, crossings = row_cuts(rows, TURNS), row_cuts(rows, CROSSINGS)
    done = {}

    def after(name, value):
        waits = AFTER.get(name, ())
        if not waits:
            return value
        value, held = lax.optimization_barrier((value, [done[w] for w in waits]))
        done.update(zip(waits, held))
        return value

    def held(name):
        return [done[w] for w in AFTER.get(name, ())]

    def move(name, value, how, *args):
        done[name] = how(after(name, value), *args)
        return done[name]

    def weight_of(owner):
        return lax.dynamic_slice_in_dim(base_weight, owner * depth, depth, 0)

    move("swap", activations, send, SWAP)
    eighths = jnp.stack([far_in * 8 + spot, far_out * 8 + spot]).astype(jnp.int32)
    move("pieces", pick(base_weight, eighths, piece), send, IN)
    partial_value = dot(activations, basis_down)

    move("across", adapter_cores, swap_rep, 2)
    move("mate", adapter_cores, swap_rep, 1)
    done["own"] = dot(after("own", activations), weight_of(me))
    move("corner", done["across"], swap_rep, 1)

    def turn(i):
        x = activations[slice(*turns[i])]
        if i == RIDE:
            blocks = partial_value.astype(jnp.bfloat16).reshape(-1, *x.shape[:1], width)
            x = jnp.concatenate([x, *blocks], axis=1)
        move(f"turn{i}", x, send, IN + OUT)
        if i == RIDE:
            x = done[f"turn{i}"]
            blocks = jnp.split(x[:, depth:], (x.shape[1] - depth) // width, axis=1)
            done[f"turn{i}"], done["part"] = x[:, :depth], jnp.concatenate(blocks, axis=0)

    def turned(a, b):
        j = [a >= start and b <= stop for start, stop in turns].index(True)
        return done[f"turn{j}"][a - turns[j][0] : b - turns[j][0]]

    def cross(i):
        move(f"cross{i}", turned(*crossings[i]), send, SWAP)

    turn(0)
    move("near1", done["pieces"][:piece], swap_groups)
    move("far1", done["pieces"][piece:], swap_rep, 2)
    turn(1)
    done["swap dot"] = done["own"] + dot(after("swap dot", done["swap"]), weight_of(far_in))
    near = jnp.concatenate([done["pieces"][:piece], done["near1"]], axis=0)
    far = jnp.concatenate([done["pieces"][piece:], done["far1"]], axis=0)
    move("near3", near, swap_rep, 1)
    move("far3", far, swap_rep, 1)
    move("near2", near, swap_rep, 2)
    move("far2", far, swap_groups)
    cross(0)
    for i in range(2, len(turns)):
        turn(i)
    near_masks, far_masks = ((0, 4), (2, 6), (1, 5), (3, 7)), ((0, 2), (4, 6), (1, 3), (5, 7))

    cross(1)
    move("near4", done["near2"], swap_rep, 1)
    move("far4", done["far2"], swap_rep, 1)

    weights = (near, done["near2"], done["near3"], done["near4"])
    done["lent"] = lend(
        spot, [done["swap"]], weights, near_masks, "lend_near", None, held("lent"), jnp.float32
    )
    weights = (far, done["far2"], done["far3"], done["far4"])
    first = 0
    for i, count in enumerate(LENDS):
        chunks = range(first, first + count)
        first += count
        if i == len(LENDS) - 1:
            cores = (adapter_cores, done["mate"], done["across"], done["corner"])
            mixed = mix(rep, row_adapter, jnp.where(inner, coded, done["coded"]), cores, held("mix"))
            done["base"] = done["swap dot"] + dot(mixed, basis_up)
        xs, add = [done[f"cross{j}"] for j in chunks], done["lent"]
        add = add[crossings[chunks[0]][0] : crossings[chunks[-1]][1]]
        done[f"lend{i}"] = lend(spot, xs, weights, far_masks, "lend_far", add, held(f"lend{i}"))
        for j in range(2, len(crossings)) if i == 0 else ():
            cross(j)
        if i == 0:
            side = done["part"].astype(jnp.float32) + partial_value
            move("half", side.astype(jnp.bfloat16), send, SWAP)
            coded = (side + done["half"].astype(jnp.float32)).astype(jnp.bfloat16)
            move("coded", coded, send, OUT)
        if i == len(LENDS) - 1:
            x = after("turned", [done[f"turn{j}"] for j in range(len(turns))])
            x = jnp.concatenate(x, axis=0)
            owner = jnp.where(inner, near_out, near_in)
            last = done["base"] + dot(x, weight_of(owner))
        move(f"back{i}", done[f"lend{i}"], send, OUT)

    last_weight = weight_of(far_out)
    back = [done[f"back{i}"] for i in range(len(LENDS))]
    out = []
    first = 0
    for i, count in enumerate(LENDS):
        start = crossings[first][0]
        for a, b in crossings[first : first + count]:
            value = last[a:b] + dot(done[f"cross{len(out)}"], last_weight)
            value = value + back[i][a - start : b - start].astype(jnp.float32)
            out.append(value.astype(jnp.bfloat16))
        first += count
    return jnp.concatenate(out, axis=0)


def on_any(activations, row_adapter, base_weight, basis_down, adapter_cores, basis_up):
    width = basis_down.shape[1]
    local_count = adapter_cores.shape[0]
    owners = lax.axis_size("rep")
    all_adapters = local_count * owners
    slot_count = all_adapters * BLK
    base = dot(lax.all_gather(activations, "tp", axis=1, tiled=True), base_weight)
    partial_value = dot(activations, basis_down)
    adapter_ids = row_adapter[:, 0]
    onehot = (adapter_ids[:, None] == jnp.arange(all_adapters, dtype=jnp.int32)[None, :]).astype(
        jnp.int32
    )
    earlier = jnp.cumsum(onehot, axis=0) - onehot
    within = jnp.sum(earlier * onehot, axis=1)
    slot_index = adapter_ids * BLK + within
    coded = lax.psum(partial_value, "tp").astype(jnp.bfloat16)
    packed = jnp.zeros((slot_count, width), jnp.bfloat16).at[slot_index].set(coded)
    packed = packed.reshape(owners, local_count, BLK, width)
    mixed_slots = jnp.einsum(
        "nasr,arq->nasq",
        lax.all_to_all(packed, "rep", split_axis=0, concat_axis=0, tiled=True),
        adapter_cores,
        preferred_element_type=jnp.float32,
    ).astype(jnp.bfloat16)
    returned = lax.all_to_all(mixed_slots, "rep", split_axis=0, concat_axis=0, tiled=True).reshape(
        slot_count, width
    )
    mixed = returned[slot_index]
    return (base + dot(mixed, basis_up)).astype(jnp.bfloat16)


def solution(mesh):
    placed = (
        P(("groups", "rep"), "tp"),
        P(("groups", "rep"), None),
        P(None, "tp"),
        P("tp", None),
        P("rep", None, None),
        P(None, "tp"),
    )
    short = (mesh.shape["groups"], mesh.shape["rep"], mesh.shape["tp"]) == (2, 4, 4)
    return jax.shard_map(
        on_line if short else on_any,
        mesh=mesh,
        in_specs=placed,
        out_specs=P(("groups", "rep"), "tp"),
        check_vma=False,
    )
```

```python
import functools

import jax
import jax.numpy as jnp
from jax import lax
from jax.experimental import pallas as pl
from jax.experimental.pallas import tpu as pltpu
from jax.sharding import PartitionSpec as P

BLK = 16


def dot(a, b):
    return jnp.dot(a, b, preferred_element_type=jnp.float32)


def mix_kernel(rep_ref, ids_ref, coded_ref, *rest):
    cores, (mixed_ref, slots_ref) = rest[:4], rest[-2:]
    rows = coded_ref.shape[0]
    each = cores[0].shape[0]
    adapters = each * len(cores)
    ids = ids_ref[...] ^ (rep_ref[0] * each)
    named = ids == lax.broadcasted_iota(jnp.int32, (rows, adapters), 1)
    below = lax.broadcasted_iota(jnp.int32, (rows, rows), 0) > lax.broadcasted_iota(
        jnp.int32, (rows, rows), 1
    )
    earlier = dot(below.astype(jnp.bfloat16), named.astype(jnp.bfloat16))
    within = jnp.sum(jnp.where(named, earlier, 0.0), axis=1, keepdims=True).astype(jnp.int32)
    slot = ids * BLK + within
    place = (slot == lax.broadcasted_iota(jnp.int32, (rows, adapters * BLK), 1)).astype(
        jnp.bfloat16
    )
    packed = lax.dot_general(
        place, coded_ref[...], (((0,), (0,)), ((), ())), preferred_element_type=jnp.float32
    ).astype(jnp.bfloat16)
    for a in range(adapters):
        slots_ref[a * BLK : (a + 1) * BLK, :] = dot(
            packed[a * BLK : (a + 1) * BLK, :], cores[a // each][a % each]
        ).astype(jnp.bfloat16)
    mixed_ref[...] = dot(place, slots_ref[...]).astype(jnp.bfloat16)


def mix(rep, ids, coded, cores, waits):
    rows, width = coded.shape
    adapters = sum(c.shape[0] for c in cores)
    return pl.pallas_call(
        mix_kernel,
        out_shape=jax.ShapeDtypeStruct((rows, width), jnp.bfloat16),
        in_specs=[pl.BlockSpec(memory_space=pltpu.SMEM)]
        + [pl.BlockSpec(memory_space=pltpu.VMEM)] * (2 + len(cores))
        + [pl.BlockSpec(memory_space=pl.ANY)] * len(waits),
        scratch_shapes=[pltpu.VMEM((adapters * BLK, width), jnp.bfloat16)],
        compiler_params=pltpu.CompilerParams(vmem_limit_bytes=10 * 2**20),
        cost_estimate=pl.CostEstimate(
            flops=2 * rows * width * (3 * adapters * BLK),
            bytes_accessed=adapters * width * width * 2 + rows * width * 4,
            transcendentals=0,
        ),
        name="mix",
    )(rep.reshape(1), ids, coded, *cores, *waits)


def pick_kernel(which_ref, x_ref, out_ref):
    out_ref[...] = x_ref[...]


def pick(x, blocks, rows, steps=4):
    columns, part = x.shape[1], rows // steps
    return pl.pallas_call(
        pick_kernel,
        out_shape=jax.ShapeDtypeStruct((blocks.size * rows, columns), x.dtype),
        grid_spec=pltpu.PrefetchScalarGridSpec(
            num_scalar_prefetch=1,
            grid=(blocks.size, steps),
            in_specs=[pl.BlockSpec((part, columns), lambda i, k, which: (which[i] * steps + k, 0))],
            out_specs=pl.BlockSpec((part, columns), lambda i, k, which: (i * steps + k, 0)),
        ),
        cost_estimate=pl.CostEstimate(
            flops=0, bytes_accessed=4 * blocks.size * rows * columns, transcendentals=0
        ),
        name="pick",
    )(blocks, x)


def lend_kernel(spot_ref, *refs, count, blocks, width, added):
    xs, rest = refs[:count], refs[count:]
    out_ref = rest[-1]
    piece = xs[0].shape[1] // sum(len(masks) for _, masks in blocks)
    spot = spot_ref[0]
    start = 0
    for x_ref in xs:
        rows = slice(start, start + x_ref.shape[0])
        start = rows.stop
        columns = [
            jnp.concatenate(
                [x_ref[:, pl.ds(pl.multiple_of((spot ^ m) * piece, piece), piece)] for m in masks],
                axis=1,
            )
            for _, masks in blocks
        ]
        for n in range(0, out_ref.shape[1], width):
            part = slice(n, n + width)
            value = rest[len(blocks)][rows, part] if added else 0.0
            for x, (operand, _) in zip(columns, blocks):
                value = value + dot(x, rest[operand][:, part])
            out_ref[rows, part] = value.astype(out_ref.dtype)


def lend(spot, xs, weights, masks, name, add=None, waits=(), dtype=jnp.bfloat16):
    rows, depth = sum(x.shape[0] for x in xs), xs[0].shape[1]
    columns = weights[0].shape[1]
    whole = pl.BlockSpec(memory_space=pltpu.VMEM)
    operands = (*xs, *weights, *(() if add is None else (add,)))
    return pl.pallas_call(
        functools.partial(
            lend_kernel,
            count=len(xs),
            blocks=tuple(enumerate(masks)),
            width=256,
            added=add is not None,
        ),
        out_shape=jax.ShapeDtypeStruct((rows, columns), dtype),
        in_specs=[pl.BlockSpec(memory_space=pltpu.SMEM)]
        + [whole] * len(operands)
        + [pl.BlockSpec(memory_space=pl.ANY)] * len(waits),
        out_specs=whole,
        compiler_params=pltpu.CompilerParams(vmem_limit_bytes=12 * 2**20),
        cost_estimate=pl.CostEstimate(
            flops=2 * rows * depth * columns,
            bytes_accessed=depth * columns * 2 + rows * (depth + columns) * 2,
            transcendentals=0,
        ),
        name=name,
    )(spot.reshape(1), *operands, *waits)


IN = [(0, 1), (3, 2)]
OUT = [(1, 0), (2, 3)]
SWAP = [(1, 2), (2, 1)]

TURNS = (4, 2, 2)
CROSSINGS = (4, 2, 2)
LENDS = (1, 1, 1)
RIDE = 1
AFTER = {
    "corner": ("mate", "own"),
    "near1": ("corner",),
    "far1": ("corner",),
    "near2": ("near3", "far3"),
    "far2": ("far3",),
    "turn1": ("far1",),
    "turn2": ("turn1",),
    "cross0": ("far1", "near1"),
    "near4": ("cross0", "turn1"),
    "far4": ("cross0", "turn1"),
    "lend1": ("lend0", "back0"),
    "lend2": ("lend1",),
    "mix": ("lend0",),
    "lent": ("far4",),
    "half": ("lent", "cross0"),
    "turned": ("lend2",),
    "cross2": ("lend0",),
    "swap dot": ("turn0",),
    "cross1": ("cross0",),
}


def send(x, pairs):
    return lax.ppermute(x, "tp", pairs)


def swap_rep(x, bit):
    return lax.ppermute(x, "rep", [(i, i ^ bit) for i in range(4)])


def swap_groups(x):
    return lax.ppermute(x, "groups", [(0, 1), (1, 0)])


def row_cuts(rows, eighths):
    ends = [0]
    for e in eighths:
        ends.append(ends[-1] + e * rows // 8)
    return list(zip(ends, ends[1:]))


def on_line(activations, row_adapter, base_weight, basis_down, adapter_cores, basis_up):
    me, rep = lax.axis_index("tp"), lax.axis_index("rep")
    inner = (me == 1) | (me == 2)
    left = me < 2
    near_in, far_in = jnp.where(left, 1, 2), jnp.where(left, 2, 1)
    near_out, far_out = jnp.where(left, 0, 3), jnp.where(left, 3, 0)
    spot = lax.axis_index("groups") * 4 + rep
    rows, depth = activations.shape
    width = basis_up.shape[0]
    piece = depth // 8
    turns, crossings = row_cuts(rows, TURNS), row_cuts(rows, CROSSINGS)
    done = {}

    def after(name, value):
        waits = AFTER.get(name, ())
        if not waits:
            return value
        value, held = lax.optimization_barrier((value, [done[w] for w in waits]))
        done.update(zip(waits, held))
        return value

    def held(name):
        return [done[w] for w in AFTER.get(name, ())]

    def move(name, value, how, *args):
        done[name] = how(after(name, value), *args)
        return done[name]

    def weight_of(owner):
        return lax.dynamic_slice_in_dim(base_weight, owner * depth, depth, 0)

    move("swap", activations, send, SWAP)
    eighths = jnp.stack([far_in * 8 + spot, far_out * 8 + spot]).astype(jnp.int32)
    move("pieces", pick(base_weight, eighths, piece), send, IN)
    partial_value = dot(activations, basis_down)

    move("across", adapter_cores, swap_rep, 2)
    move("mate", adapter_cores, swap_rep, 1)
    done["own"] = dot(after("own", activations), weight_of(me))
    move("corner", done["across"], swap_rep, 1)

    def turn(i):
        x = activations[slice(*turns[i])]
        if i == RIDE:
            blocks = partial_value.astype(jnp.bfloat16).reshape(-1, *x.shape[:1], width)
            x = jnp.concatenate([x, *blocks], axis=1)
        move(f"turn{i}", x, send, IN + OUT)
        if i == RIDE:
            x = done[f"turn{i}"]
            blocks = jnp.split(x[:, depth:], (x.shape[1] - depth) // width, axis=1)
            done[f"turn{i}"], done["part"] = x[:, :depth], jnp.concatenate(blocks, axis=0)

    def turned(a, b):
        j = [a >= start and b <= stop for start, stop in turns].index(True)
        return done[f"turn{j}"][a - turns[j][0] : b - turns[j][0]]

    def cross(i):
        move(f"cross{i}", turned(*crossings[i]), send, SWAP)

    turn(0)
    move("near1", done["pieces"][:piece], swap_groups)
    move("far1", done["pieces"][piece:], swap_rep, 2)
    turn(1)
    done["swap dot"] = done["own"] + dot(after("swap dot", done["swap"]), weight_of(far_in))
    near = jnp.concatenate([done["pieces"][:piece], done["near1"]], axis=0)
    far = jnp.concatenate([done["pieces"][piece:], done["far1"]], axis=0)
    move("near3", near, swap_rep, 1)
    move("far3", far, swap_rep, 1)
    move("near2", near, swap_rep, 2)
    move("far2", far, swap_groups)
    cross(0)
    for i in range(2, len(turns)):
        turn(i)
    near_masks, far_masks = ((0, 4), (2, 6), (1, 5), (3, 7)), ((0, 2), (4, 6), (1, 3), (5, 7))

    cross(1)
    move("near4", done["near2"], swap_rep, 1)
    move("far4", done["far2"], swap_rep, 1)

    weights = (near, done["near2"], done["near3"], done["near4"])
    done["lent"] = lend(
        spot, [done["swap"]], weights, near_masks, "lend_near", None, held("lent"), jnp.float32
    )
    weights = (far, done["far2"], done["far3"], done["far4"])
    first = 0
    for i, count in enumerate(LENDS):
        chunks = range(first, first + count)
        first += count
        if i == len(LENDS) - 1:
            cores = (adapter_cores, done["mate"], done["across"], done["corner"])
            mixed = mix(rep, row_adapter, jnp.where(inner, coded, done["coded"]), cores, held("mix"))
            done["base"] = done["swap dot"] + dot(mixed, basis_up)
        xs, add = [done[f"cross{j}"] for j in chunks], done["lent"]
        add = add[crossings[chunks[0]][0] : crossings[chunks[-1]][1]]
        done[f"lend{i}"] = lend(spot, xs, weights, far_masks, "lend_far", add, held(f"lend{i}"))
        for j in range(2, len(crossings)) if i == 0 else ():
            cross(j)
        if i == 0:
            side = done["part"].astype(jnp.float32) + partial_value
            move("half", side.astype(jnp.bfloat16), send, SWAP)
            coded = (side + done["half"].astype(jnp.float32)).astype(jnp.bfloat16)
            move("coded", coded, send, OUT)
        if i == len(LENDS) - 1:
            x = after("turned", [done[f"turn{j}"] for j in range(len(turns))])
            x = jnp.concatenate(x, axis=0)
            owner = jnp.where(inner, near_out, near_in)
            last = done["base"] + dot(x, weight_of(owner))
        move(f"back{i}", done[f"lend{i}"], send, OUT)

    last_weight = weight_of(far_out)
    back = [done[f"back{i}"] for i in range(len(LENDS))]
    out = []
    first = 0
    for i, count in enumerate(LENDS):
        start = crossings[first][0]
        for a, b in crossings[first : first + count]:
            value = last[a:b] + dot(done[f"cross{len(out)}"], last_weight)
            value = value + back[i][a - start : b - start].astype(jnp.float32)
            out.append(value.astype(jnp.bfloat16))
        first += count
    return jnp.concatenate(out, axis=0)


def on_any(activations, row_adapter, base_weight, basis_down, adapter_cores, basis_up):
    width = basis_down.shape[1]
    local_count = adapter_cores.shape[0]
    owners = lax.axis_size("rep")
    all_adapters = local_count * owners
    slot_count = all_adapters * BLK
    base = dot(lax.all_gather(activations, "tp", axis=1, tiled=True), base_weight)
    partial_value = dot(activations, basis_down)
    adapter_ids = row_adapter[:, 0]
    onehot = (adapter_ids[:, None] == jnp.arange(all_adapters, dtype=jnp.int32)[None, :]).astype(
        jnp.int32
    )
    earlier = jnp.cumsum(onehot, axis=0) - onehot
    within = jnp.sum(earlier * onehot, axis=1)
    slot_index = adapter_ids * BLK + within
    coded = lax.psum(partial_value, "tp").astype(jnp.bfloat16)
    packed = jnp.zeros((slot_count, width), jnp.bfloat16).at[slot_index].set(coded)
    packed = packed.reshape(owners, local_count, BLK, width)
    mixed_slots = jnp.einsum(
        "nasr,arq->nasq",
        lax.all_to_all(packed, "rep", split_axis=0, concat_axis=0, tiled=True),
        adapter_cores,
        preferred_element_type=jnp.float32,
    ).astype(jnp.bfloat16)
    returned = lax.all_to_all(mixed_slots, "rep", split_axis=0, concat_axis=0, tiled=True).reshape(
        slot_count, width
    )
    mixed = returned[slot_index]
    return (base + dot(mixed, basis_up)).astype(jnp.bfloat16)


def solution(mesh):
    placed = (
        P(("groups", "rep"), "tp"),
        P(("groups", "rep"), None),
        P(None, "tp"),
        P("tp", None),
        P("rep", None, None),
        P(None, "tp"),
    )
    short = (mesh.shape["groups"], mesh.shape["rep"], mesh.shape["tp"]) == (2, 4, 4)
    return jax.shard_map(
        on_line if short else on_any,
        mesh=mesh,
        in_specs=placed,
        out_specs=P(("groups", "rep"), "tp"),
        check_vma=False,
    )
```
